32 devices in a mesh: shot: 8 (over z, y), slab: 4 (over x, core).
Axes of the slice: x: 2, y: 2, z: 4, core: 2. Of those that a mesh axis runs over, the one named last changes fastest.
Arguments:
- forward_state: float32 [8, 9, 32, 32, 128], P('shot', None, 'slab'), may hold values from -6 to 6
- adjoint_state: float32 [8, 9, 32, 32, 128], P('shot', None, 'slab'), may hold values from -6 to 6
- materials: float32 [10, 32, 32, 128], P(None, 'slab', 'shot'), may hold values from 0.1 to 2, as said below
- wavelet: float32 [4], replicated, may hold values from -4 to 4
- encoding: int32 [8, 16], P('shot'), may hold values from 0 to 1
- source_cells: int32 [8, 16], P('shot'), may hold values from 0 to 131071
- receiver_depth: int32 [32, 32], P('slab'), may hold values from 0 to 3
- receiver_data: float32 [8, 4, 32, 32], P('shot', None, 'slab'), may hold values from -6 to 6
Outputs:
- forward_out: float32 [8, 9, 32, 32, 128], P('shot', None, 'slab')
- adjoint_out: float32 [8, 9, 32, 32, 128], P('shot', None, 'slab')
- gradient: float32 [10, 32, 32, 128], P(None, 'slab', 'shot')
The draws below stay inside these ranges and needn't reach their ends.
Inputs may be any that keep to these rules, and one draw needn't show every extreme that they name: `materials`: row 0 lies in 0.5 to 1; rows 1, 4, 6 in 1 to 2; rows 2, 3, 5 in 0.1 to 0.4; rows 7, 8, 9 in 0.3 to 1.
All inputs are finite; a program needn't handle non-finite values.
Results may differ from the reference program's by a relative error of at most 0.0001.
Values sent between devices are 32-bit elements; how exact they have to be, the bound alone decides.
A program may use at most 64 MiB of HBM per device.

```python
import jax
import jax.numpy as jnp
from jax import lax

NY = 32
NZ = 128
NSRC = 16
STEPS = 4
SHOTS = 8
NX = 32


def draw_materials(key, part):
    lower_ends = jnp.array([0.5, 1.0, 0.1, 0.1, 1.0, 0.1, 1.0, 0.3, 0.3, 0.3], jnp.float32)[:, None, None, None]
    upper_ends = jnp.array([1.0, 2.0, 0.4, 0.4, 2.0, 0.4, 2.0, 1.0, 1.0, 1.0], jnp.float32)[:, None, None, None]
    uniform_draw = jax.random.uniform(key, (10, NX, NY, NZ), jnp.float32)
    return lower_ends * (upper_ends / lower_ends) ** uniform_draw


def touch_ends(result, key, low, high):
    index_at = [jax.random.randint(jax.random.fold_in(key, axis), (), 0, length) for axis, length in enumerate(result.shape)]
    widest = result.shape.index(max(result.shape))
    neighbour = index_at[:widest] + [(index_at[widest] + 1) % result.shape[widest]] + index_at[widest + 1:]
    return result.at[tuple(index_at)].set(low).at[tuple(neighbour)].set(high)


def level_of(key, shape, pieces, least, top_value):
    level, own = 1.0, jax.random.fold_in(key, 6)
    for axis_at, parts in pieces:
        draws = jnp.exp(jax.random.uniform(jax.random.fold_in(own, axis_at), (parts,), jnp.float32, least / len(pieces), top_value / len(pieces)))
        level = level * jnp.repeat(draws, shape[axis_at] // parts).reshape([-1 if axis == axis_at else 1 for axis in range(len(shape))])
    return level


def centred(own_key, shape, deviation, reach, pieces=(), held_as=jnp.bfloat16):
    result = jax.random.normal(own_key, shape, jnp.float32) * deviation
    if len(pieces) > 0:
        result = level_of(own_key, shape, pieces, -0.22, 0.18) * result
    return jnp.clip(result, min=-reach, max=reach).astype(held_as)


def setup_inputs(seed: int = 0) -> dict:
    splits = jax.random.split(jax.random.key(seed), 9)
    return {
        "forward_state": centred(splits[0], (SHOTS, 9, NX, NY, NZ), 1.0, 6.0, ((0, 8), (2, 4)), jnp.float32),
        "adjoint_state": centred(splits[1], (SHOTS, 9, NX, NY, NZ), 1.0, 6.0, ((0, 8), (2, 4)), jnp.float32),
        "materials": draw_materials(jax.random.fold_in(splits[8], 71), 0),
        "wavelet": centred(splits[3], (STEPS,), 1.0, 4.0, (), jnp.float32),
        "encoding": touch_ends(jax.random.randint(splits[4], (SHOTS, NSRC), 0, 2), jax.random.fold_in(splits[4], 1), 0, 1).astype(jnp.int32),
        "source_cells": touch_ends(jax.random.randint(splits[5], (SHOTS, NSRC), 0, NX * NY * NZ), jax.random.fold_in(splits[5], 1), 0, (NX * NY * NZ) - 1).astype(jnp.int32),
        "receiver_depth": touch_ends(jax.random.randint(splits[6], (NX, NY), 0, 4), jax.random.fold_in(splits[6], 1), 0, 3).astype(jnp.int32),
        "receiver_data": centred(splits[7], (SHOTS, STEPS, NX, NY), 1.0, 6.0, ((0, 8), (2, 4)), jnp.float32),
    }


step_size = 0.25


def diff_up(values, direction):
    length = values.shape[direction]
    ahead = lax.slice_in_dim(values, 1, length, axis=direction)
    zero_layer = jnp.zeros_like(lax.slice_in_dim(values, 0, 1, axis=direction))
    return jnp.concatenate([ahead, zero_layer], axis=direction) - values


def diff_down(values, direction):
    length = values.shape[direction]
    behind = lax.slice_in_dim(values, 0, length - 1, axis=direction)
    zero_layer = jnp.zeros_like(lax.slice_in_dim(values, 0, 1, axis=direction))
    return values - jnp.concatenate([zero_layer, behind], axis=direction)


def velocity_forces(stress, dx_sxx, dx_sxy, dx_sxz):
    force_x = dx_sxx + diff_down(stress[:, 5], 2) + diff_down(stress[:, 4], 3)
    force_y = dx_sxy + diff_up(stress[:, 1], 2) + diff_down(stress[:, 3], 3)
    force_z = dx_sxz + diff_down(stress[:, 3], 2) + diff_up(stress[:, 2], 3)
    return jnp.stack([force_x, force_y, force_z], axis=1)


def strains(velocity, dx_vx, dx_vy, dx_vz):
    strain_xx = dx_vx
    strain_yy = diff_down(velocity[:, 1], 2)
    strain_zz = diff_down(velocity[:, 2], 3)
    strain_yz = diff_up(velocity[:, 1], 3) + diff_up(velocity[:, 2], 2)
    strain_xz = diff_up(velocity[:, 0], 3) + dx_vz
    strain_xy = diff_up(velocity[:, 0], 2) + dx_vy
    return [strain_xx, strain_yy, strain_zz, strain_yz, strain_xz, strain_xy]


def stress_rates(strain, stiffness):
    strain_xx, strain_yy, strain_zz, strain_yz, strain_xz, strain_xy = strain
    return jnp.stack([
        stiffness[0] * strain_xx + stiffness[1] * strain_yy + stiffness[2] * strain_zz,
        stiffness[1] * strain_xx + stiffness[3] * strain_yy + stiffness[4] * strain_zz,
        stiffness[2] * strain_xx + stiffness[4] * strain_yy + stiffness[5] * strain_zz,
        stiffness[6] * strain_yz,
        stiffness[7] * strain_xz,
        stiffness[8] * strain_xy], axis=1)


def correlate(buoy_grad, strain, halfway):
    forward = [part[:halfway] for part in strain]
    adjoint = [part[halfway:] for part in strain]
    pairs = [(0, 0), (0, 1), (0, 2), (1, 1), (1, 2), (2, 2), (3, 3), (4, 4), (5, 5)]
    terms = [buoy_grad]
    for first, second in pairs:
        product = forward[first] * adjoint[second]
        if first != second:
            product = product + forward[second] * adjoint[first]
        terms.append(jnp.sum(product, axis=0))
    return jnp.stack(terms)


def reference(forward_state, adjoint_state, materials, wavelet, encoding, source_cells, receiver_depth, receiver_data):
    cell_count = NX * NY * NZ
    probe = (lax.broadcasted_iota(jnp.int32, (NX, NY, NZ), 2) == receiver_depth[:, :, None]).astype(jnp.float32)
    buoyancy = materials[0]
    stiffness = materials[1:]

    def one_shot(grad_total, inputs):
        forward, adjoint, shot_code, shot_cells, shot_data = inputs
        sign_values = (2 * shot_code - 1).astype(jnp.float32)
        source_image = jnp.zeros((cell_count,), jnp.float32).at[shot_cells].add(sign_values).reshape(NX, NY, NZ)
        state = jnp.stack([forward, adjoint])
        velocity = state[:, 0:3]
        stress = state[:, 3:9]
        for step_index in range(STEPS):
            force = velocity_forces(stress, diff_up(stress[:, 0], 1), diff_down(stress[:, 5], 1), diff_down(stress[:, 4], 1))
            buoy_grad = jnp.sum(force[0:1] * velocity[1:2], axis=(0, 1))
            velocity = velocity + step_size * buoyancy * force
            strain = strains(velocity, diff_down(velocity[:, 0], 1), diff_up(velocity[:, 1], 1), diff_up(velocity[:, 2], 1))
            stress = stress + step_size * stress_rates(strain, stiffness)
            inject = jnp.stack([wavelet[step_index] * source_image, shot_data[step_index][:, :, None] * probe])
            stress = stress.at[:, 2].add(inject)
            grad_total = grad_total + correlate(buoy_grad, strain, 1)
        state = jnp.concatenate([velocity, stress], axis=1)
        return grad_total, (state[0], state[1])

    start = jnp.zeros((10, NX, NY, NZ), jnp.float32)
    grad_total, outputs = lax.scan(one_shot, start, (forward_state, adjoint_state, encoding, source_cells, receiver_data))
    gradient = grad_total * (float(SHOTS * STEPS) ** -0.5)
    return outputs[0], outputs[1], gradient
```

```python
import functools

import jax
import jax.numpy as jnp
from jax import lax
from jax.experimental import pallas as pl
from jax.experimental.pallas import tpu as pltpu
from jax.sharding import PartitionSpec as P

STEPS = 4
STEP_SIZE = 0.25
VX, VY, VZ, SXX, SYY, SZZ, SYZ, SXZ, SXY = range(9)
PAIRS = [(0, 0), (0, 1), (0, 2), (1, 1), (1, 2), (2, 2), (3, 3), (4, 4), (5, 5)]


def kernel(
    n,
    slabs,
    scale,
    wavelet,
    encoding,
    cells,
    depth,
    data,
    fwd_in,
    adj_in,
    mats_in,
    fwd_out,
    adj_out,
    grad_out,
    F,
    slots,
    mat,
    acc,
    image,
    inj,
    blocks,
    ry,
    rright,
    rleft,
    load_sem,
    store_sem,
    halo_send,
    halo_recv,
    ag_recv,
    ag_send_z,
    ag_send_o,
    ag_send_y,
    rs_recv_y,
    rs_send_y,
    rs_recv_r,
    rs_send_r,
    rs_recv_l,
    rs_send_l,
):
    _, comps, xr, ny, nz = fwd_in.shape
    yb = mats_in.shape[2]
    nc = mats_in.shape[0]
    L = n // 2
    me = lax.axis_index("shot")
    slab = lax.axis_index("slab")
    lo = lax.rem(me, 2)
    hi = me // 2
    partner = hi * 2 + 1 - lo

    loads = [
        pltpu.make_async_copy(fwd_in.at[0], F.at[0, :, pl.ds(1, xr)], load_sem.at[0]),
        pltpu.make_async_copy(adj_in.at[0], F.at[1, :, pl.ds(1, xr)], load_sem.at[1]),
        pltpu.make_async_copy(mats_in, slots.at[me], load_sem.at[2]),
    ]
    for c in loads:
        c.start()
    zero_layer = jnp.zeros((ny, nz), jnp.float32)
    for w in range(2):
        for c in (VX, SXZ, SXY):
            F[w, c, 0] = zero_layer
        for c in (VY, VZ, SXX):
            F[w, c, xr + 1] = zero_layer

    def shot_id(index):
        return {"shot": index}

    def slab_id(index):
        return {"slab": index}

    MESH = pl.DeviceIdType.MESH
    barrier = pltpu.get_barrier_semaphore()

    def greet(cond, device):
        @pl.when(cond)
        def _():
            pl.semaphore_signal(barrier, inc=1, device_id=device, device_id_type=MESH)

    has_r = hi < L - 1
    has_l = hi > 0
    has_up = slab < slabs - 1
    has_dn = slab > 0
    pl.semaphore_signal(barrier, inc=1, device_id=shot_id(partner), device_id_type=MESH)
    greet(has_r, shot_id(me + 2))
    greet(has_l, shot_id(me - 2))
    greet(has_up, slab_id(slab + 1))
    greet(has_dn, slab_id(slab - 1))
    one = jnp.int32(1)
    nul = jnp.int32(0)
    count = (
        one
        + jnp.where(has_r, one, nul)
        + jnp.where(has_l, one, nul)
        + jnp.where(has_up, one, nul)
        + jnp.where(has_dn, one, nul)
    )
    pl.semaphore_wait(barrier, count)

    def remote(src, dst, ss, rs, device):
        return pltpu.make_async_remote_copy(
            src_ref=src,
            dst_ref=dst,
            send_sem=ss,
            recv_sem=rs,
            device_id=device,
            device_id_type=MESH,
        )

    def when(cond, fn):
        pl.when(cond)(fn)

    def to_partner(block, src):
        return remote(
            src, slots.at[block], ag_send_y.at[block // 2], ag_recv.at[block], shot_id(partner)
        )

    def to_line(block, src, by, sem):
        return remote(src, slots.at[block], sem, ag_recv.at[block], shot_id(me + 2 * by))

    own_r = to_line(me, mats_in, 1, ag_send_z.at[me])
    own_l = to_line(me, mats_in, -1, ag_send_o.at[0])
    own_p = to_partner(me, mats_in)
    when(has_r, own_r.start)
    when(has_l, own_l.start)
    own_p.start()

    def halo(kind, t):
        if kind == 0:
            up_src, up_dst = F.at[:, pl.ds(SXZ, 2), xr], F.at[:, pl.ds(SXZ, 2), 0]
            dn_src, dn_dst = F.at[:, SXX, 1], F.at[:, SXX, xr + 1]
        else:
            up_src, up_dst = F.at[:, VX, xr], F.at[:, VX, 0]
            dn_src, dn_dst = F.at[:, pl.ds(VY, 2), 1], F.at[:, pl.ds(VY, 2), xr + 1]
        up = remote(
            up_src, up_dst, halo_send.at[0, kind, t], halo_recv.at[0, kind, t], slab_id(slab + 1)
        )
        dn = remote(
            dn_src, dn_dst, halo_send.at[1, kind, t], halo_recv.at[1, kind, t], slab_id(slab - 1)
        )
        return up, dn

    def halo_start(kind, t):
        up, dn = halo(kind, t)
        when(has_up, up.start)
        when(has_dn, dn.start)

    def halo_wait(kind, t):
        up, dn = halo(kind, t)
        when(has_dn, up.wait_recv)
        when(has_up, dn.wait_recv)

    def halo_sent(kind, t):
        up, dn = halo(kind, t)
        when(has_up, up.wait_send)
        when(has_dn, dn.wait_send)

    for c in loads:
        c.wait()
    halo_start(0, 0)

    lane = lax.broadcasted_iota(jnp.int32, (ny, nz), 1)
    row = lax.broadcasted_iota(jnp.int32, (ny, nz), 0)

    eye = lax.broadcasted_iota(jnp.int32, (ny, ny), 0) == lax.broadcasted_iota(
        jnp.int32, (ny, ny), 1
    )

    def column(r):
        wide = jnp.broadcast_to(r, (ny, ny))
        return jnp.sum(jnp.where(eye, wide, 0.0), axis=1, keepdims=True)

    def prepare(x, carry):
        cell = ((slab * xr + x) * ny + row) * nz + lane
        total = jnp.zeros((ny, nz), jnp.float32)
        for j in range(cells.shape[1]):
            sign = (2 * encoding[0, j] - 1).astype(jnp.float32)
            total = total + jnp.where(cell == cells[0, j], sign, 0.0)
        image[x] = total
        hit = lane.astype(jnp.float32) == column(depth[pl.ds(x, 1), :].astype(jnp.float32))
        for t in range(STEPS):
            inj[t, x] = jnp.where(hit, column(data[0, t, pl.ds(x, 1), :]), 0.0)
        return carry

    lax.fori_loop(0, xr, prepare, 0)

    for k in range(1, L):
        def right_moving(k=k):
            b = me - 2 * k
            ref = slots.at[b]
            to_line(b, ref, 1, ag_send_z.at[b]).wait_recv()
            when(has_r, to_line(b, ref, 1, ag_send_z.at[b]).start)
            to_partner(b, ref).start()

        def left_moving(k=k):
            b = me + 2 * k
            ref = slots.at[b]
            to_line(b, ref, -1, ag_send_z.at[b]).wait_recv()
            when(has_l, to_line(b, ref, -1, ag_send_z.at[b]).start)
            to_partner(b, ref).start()

        when(hi >= k, right_moving)
        when(hi + k < L, left_moving)
    for h in range(L):
        b = h * 2 + 1 - lo
        to_partner(b, slots.at[b]).wait_recv()

    def assemble(x, carry):
        for c in range(nc):
            whole = jnp.concatenate([slots[i, c, x] for i in range(n)], axis=0)
            mat[c, x + 1] = whole * STEP_SIZE
        return carry

    lax.fori_loop(0, xr, assemble, 0)

    def up_y(a):
        return jnp.where(row == ny - 1, 0.0, pltpu.roll(a, ny - 1, 0)) - a

    def down_y(a):
        return a - jnp.where(row == 0, 0.0, pltpu.roll(a, 1, 0))

    def up_z(a):
        return jnp.where(lane == nz - 1, 0.0, pltpu.roll(a, nz - 1, 1)) - a

    def down_z(a):
        return a - jnp.where(lane == 0, 0.0, pltpu.roll(a, 1, 1))

    def velocity_layer(t, x):
        forces = []
        old = []
        for w in range(2):
            sxx, sxy, sxz = F[w, SXX, x], F[w, SXY, x], F[w, SXZ, x]
            syz = F[w, SYZ, x]
            fx = (F[w, SXX, x + 1] - sxx) + down_y(sxy) + down_z(sxz)
            fy = (sxy - F[w, SXY, x - 1]) + up_y(F[w, SYY, x]) + down_z(syz)
            fz = (sxz - F[w, SXZ, x - 1]) + down_y(syz) + up_z(F[w, SZZ, x])
            forces.append([fx, fy, fz])
            old.append([F[w, VX, x], F[w, VY, x], F[w, VZ, x]])
        term = (
            forces[0][0] * old[1][0] + forces[0][1] * old[1][1] + forces[0][2] * old[1][2]
        )
        acc[0, x] = term if t == 0 else acc[0, x] + term
        buoy = mat[0, x]
        for w in range(2):
            for c in range(3):
                F[w, c, x] = old[w][c] + buoy * forces[w][c]

    def strain_of(w, x):
        vx, vy, vz = F[w, VX, x], F[w, VY, x], F[w, VZ, x]
        return [
            vx - F[w, VX, x - 1],
            down_y(vy),
            down_z(vz),
            up_z(vy) + up_y(vz),
            up_z(vx) + (F[w, VZ, x + 1] - vz),
            up_y(vx) + (F[w, VY, x + 1] - vy),
        ]

    def add_terms(t, x, f, a, last):
        for i, (p, q) in enumerate(PAIRS):
            term = f[p] * a[q]
            if p != q:
                term = term + f[q] * a[p]
            if t > 0:
                term = term + acc[i + 1, x]
            if last:
                put_block(i + 1, x, term)
            else:
                acc[i + 1, x] = term

    def put_block(c, x, total):
        total = total * scale
        for i in range(n):
            blocks[i, c, x - 1] = total[i * yb : (i + 1) * yb]

    def stress_layer(t, x, strains):
        m = [mat[c, x] for c in range(nc)]
        for w in range(2):
            exx, eyy, ezz, gyz, gxz, gxy = strains[w]
            F[w, SXX, x] = F[w, SXX, x] + (m[1] * exx + m[2] * eyy + m[3] * ezz)
            F[w, SYY, x] = F[w, SYY, x] + (m[2] * exx + m[4] * eyy + m[5] * ezz)
            extra = wavelet[t] * image[x - 1] if w == 0 else inj[t, x - 1]
            F[w, SZZ, x] = F[w, SZZ, x] + (m[3] * exx + m[5] * eyy + m[6] * ezz) + extra
            F[w, SYZ, x] = F[w, SYZ, x] + m[7] * gyz
            F[w, SXZ, x] = F[w, SXZ, x] + m[8] * gxz
            F[w, SXY, x] = F[w, SXY, x] + m[9] * gxy

    def over(start, stop, step, fn):
        def one_layer(j, carry):
            fn(start + j * step)
            return carry

        lax.fori_loop(0, (stop - start + step - 1) // step, one_layer, 0)

    def interior(fn):
        over(2, xr, 1, fn)

    def rims(fn):
        over(1, xr + 1, xr - 1, fn)

    stores = []

    def store(first, count, sem):
        for w, out in ((0, fwd_out), (1, adj_out)):
            c = pltpu.make_async_copy(
                F.at[w, pl.ds(first, count), pl.ds(1, xr)],
                out.at[0, pl.ds(first, count)],
                store_sem.at[sem, w],
            )
            c.start()
            stores.append(c)

    for t in range(STEPS):
        last = t == STEPS - 1
        interior(functools.partial(velocity_layer, t))
        halo_wait(0, t)
        if t > 0:
            halo_sent(1, t - 1)
        rims(functools.partial(velocity_layer, t))
        halo_start(1, t)

        def both(x, t=t, last=last):
            strains = [strain_of(w, x) for w in range(2)]
            add_terms(t, x, strains[0], strains[1], last)
            if not last:
                stress_layer(t, x, strains)

        interior(both)
        halo_wait(1, t)
        halo_sent(0, t)
        rims(both)
        if not last:
            halo_start(0, t + 1)
    halo_sent(1, STEPS - 1)
    store(0, 3, 0)
    over(1, xr + 1, 1, lambda x: put_block(0, x, acc[0, x]))

    def rs_y(d):
        return remote(
            blocks.at[d * 2 + 1 - lo],
            ry.at[d],
            rs_send_y.at[d],
            rs_recv_y.at[d],
            shot_id(partner),
        )

    def rs_r(d):
        return remote(
            ry.at[d], rright.at[d], rs_send_r.at[d], rs_recv_r.at[d], shot_id(me + 2)
        )

    def rs_l(d):
        return remote(ry.at[d], rleft.at[d], rs_send_l.at[d], rs_recv_l.at[d], shot_id(me - 2))

    for k in range(L - 1, 0, -1):
        when(hi + k < L, lambda k=k: rs_y(hi + k).start())
        when(hi >= k, lambda k=k: rs_y(hi - k).start())
    rs_y(hi).start()

    over(1, xr + 1, 1, lambda x: stress_layer(STEPS - 1, x, [strain_of(w, x) for w in range(2)]))
    store(3, comps - 3, 1)

    def add_into(d, extra):
        def one_layer(x, carry):
            for c in range(nc):
                total = ry[d, c, x] + blocks[d * 2 + lo, c, x]
                if extra is not None:
                    total = total + extra[d, c, x]
                ry[d, c, x] = total
            return carry

        lax.fori_loop(0, xr, one_layer, 0)

    for k in range(L - 1, 0, -1):
        def send_right(k=k):
            d = hi + k
            rs_y(d).wait_recv()

            def plus():
                rs_r(d).wait_recv()
                add_into(d, rright)

            when(has_l, plus)
            when(hi == 0, lambda: add_into(d, None))
            rs_r(d).start()

        def send_left(k=k):
            d = hi - k
            rs_y(d).wait_recv()

            def plus():
                rs_l(d).wait_recv()
                add_into(d, rleft)

            when(has_r, plus)
            when(hi == L - 1, lambda: add_into(d, None))
            rs_l(d).start()

        when(hi + k < L, send_right)
        when(hi >= k, send_left)

    rs_y(hi).wait_recv()
    add_into(hi, None)

    def take(ref):
        def one_layer(x, carry):
            for c in range(nc):
                ry[hi, c, x] = ry[hi, c, x] + ref[hi, c, x]
            return carry

        lax.fori_loop(0, xr, one_layer, 0)

    def from_left():
        rs_r(hi).wait_recv()
        take(rright)

    def from_right():
        rs_l(hi).wait_recv()
        take(rleft)

    when(has_l, from_left)
    when(has_r, from_right)
    final = pltpu.make_async_copy(ry.at[hi], grad_out, load_sem.at[2])
    final.start()

    when(has_r, own_r.wait_send)
    when(has_l, own_l.wait_send)
    own_p.wait_send()
    for k in range(1, L):
        def right_sent(k=k):
            b = me - 2 * k
            when(has_r, to_line(b, slots.at[b], 1, ag_send_z.at[b]).wait_send)
            to_partner(b, slots.at[b]).wait_send()

        def left_sent(k=k):
            b = me + 2 * k
            when(has_l, to_line(b, slots.at[b], -1, ag_send_z.at[b]).wait_send)
            to_partner(b, slots.at[b]).wait_send()

        when(hi >= k, right_sent)
        when(hi + k < L, left_sent)
        when(hi + k < L, lambda k=k: rs_y(hi + k).wait_send())
        when(hi >= k, lambda k=k: rs_y(hi - k).wait_send())
        when(hi + k < L, lambda k=k: rs_r(hi + k).wait_send())
        when(hi >= k, lambda k=k: rs_l(hi - k).wait_send())
    rs_y(hi).wait_send()
    for c in stores:
        c.wait()
    final.wait()


def solution(mesh):
    n = mesh.shape["shot"]
    slabs = mesh.shape["slab"]

    def body(fwd, adj, mats, wavelet, encoding, cells, depth, data):
        shots, comps, xr, ny, nz = fwd.shape
        nc, _, yb, _ = mats.shape
        L = n // 2
        scale = float(shots * n * STEPS) ** (-0.5)
        any_spec = pl.BlockSpec(memory_space=pl.ANY)
        smem = pl.BlockSpec(memory_space=pltpu.SMEM)
        vmem = pl.BlockSpec(memory_space=pltpu.VMEM)
        dma = pltpu.SemaphoreType.DMA
        f32 = jnp.float32
        return pl.pallas_call(
            functools.partial(kernel, n, slabs, scale),
            out_shape=(
                jax.ShapeDtypeStruct(fwd.shape, f32),
                jax.ShapeDtypeStruct(adj.shape, f32),
                jax.ShapeDtypeStruct(mats.shape, f32),
            ),
            in_specs=[smem, smem, smem, vmem, vmem, any_spec, any_spec, any_spec],
            out_specs=(any_spec, any_spec, any_spec),
            scratch_shapes=[
                pltpu.VMEM((2, comps, xr + 2, ny, nz), f32),
                pltpu.VMEM((n, nc, xr, yb, nz), f32),
                pltpu.VMEM((nc, xr + 2, ny, nz), f32),
                pltpu.VMEM((nc, xr + 2, ny, nz), f32),
                pltpu.VMEM((xr, ny, nz), f32),
                pltpu.VMEM((STEPS, xr, ny, nz), f32),
                pltpu.VMEM((n, nc, xr, yb, nz), f32),
                pltpu.VMEM((L, nc, xr, yb, nz), f32),
                pltpu.VMEM((L, nc, xr, yb, nz), f32),
                pltpu.VMEM((L, nc, xr, yb, nz), f32),
                dma((3,)),
                dma((2, 2)),
                dma((2, 2, STEPS)),
                dma((2, 2, STEPS)),
                dma((n,)),
                dma((n,)),
                dma((1,)),
                dma((L,)),
                dma((L,)),
                dma((L,)),
                dma((L,)),
                dma((L,)),
                dma((L,)),
                dma((L,)),
            ],
            compiler_params=pltpu.CompilerParams(
                collective_id=0, has_side_effects=True, vmem_limit_bytes=48 * 1024 * 1024
            ),
        )(wavelet, encoding, cells, depth, data, fwd, adj, mats)

    return jax.shard_map(
        body,
        mesh=mesh,
        in_specs=(
            P("shot", None, "slab", None, None),
            P("shot", None, "slab", None, None),
            P(None, "slab", "shot", None),
            P(),
            P("shot", None),
            P("shot", None),
            P("slab", None),
            P("shot", None, "slab", None),
        ),
        out_specs=(
            P("shot", None, "slab", None, None),
            P("shot", None, "slab", None, None),
            P(None, "slab", "shot", None),
        ),
        check_vma=False,
    )
```

```python
import functools

import jax
import jax.numpy as jnp
from jax import lax
from jax.experimental import pallas as pl
from jax.experimental.pallas import tpu as pltpu
from jax.sharding import PartitionSpec as P

STEPS = 4
STEP_SIZE = 0.25
VX, VY, VZ, SXX, SYY, SZZ, SYZ, SXZ, SXY = range(9)
PAIRS = [(0, 0), (0, 1), (0, 2), (1, 1), (1, 2), (2, 2), (3, 3), (4, 4), (5, 5)]


def kernel(
    n,
    slabs,
    scale,
    wavelet_in,
    encoding_in,
    cells_in,
    depth_in,
    data_in,
    fwd_in,
    adj_in,
    mats_in,
    fwd_out,
    adj_out,
    grad_out,
    wavelet,
    encoding,
    cells,
    depth,
    data,
    F,
    up_out,
    dn_out,
    up_got,
    dn_got,
    slots,
    mat,
    acc,
    image,
    inj,
    blocks,
    ry,
    rright,
    rleft,
    load_sem,
    store_sem,
    halo_send,
    halo_recv,
    ag_recv,
    ag_send_z,
    ag_send_o,
    ag_send_y,
    rs_recv_y,
    rs_send_y,
    rs_recv_r,
    rs_send_r,
    rs_recv_l,
    rs_send_l,
):
    _, comps, xr, ny, nz = fwd_in.shape
    yb = mats_in.shape[2]
    nc = mats_in.shape[0]
    L = n // 2
    me = lax.axis_index("shot")
    slab = lax.axis_index("slab")
    lo = lax.rem(me, 2)
    hi = me // 2
    partner = hi * 2 + 1 - lo

    small = [
        pltpu.make_async_copy(src, dst, load_sem.at[3 + i])
        for i, (src, dst) in enumerate(
            [
                (wavelet_in, wavelet),
                (encoding_in, encoding),
                (cells_in, cells),
                (depth_in, depth),
                (data_in, data),
            ]
        )
    ]
    loads = [
        pltpu.make_async_copy(fwd_in.at[0], F.at[0, :, pl.ds(1, xr)], load_sem.at[0]),
        pltpu.make_async_copy(adj_in.at[0], F.at[1, :, pl.ds(1, xr)], load_sem.at[1]),
        pltpu.make_async_copy(mats_in, slots.at[me], load_sem.at[2]),
    ]
    for c in loads + small:
        c.start()
    zero_layer = jnp.zeros((ny, nz), jnp.float32)
    mat[0, 0] = zero_layer
    mat[0, xr + 1] = zero_layer
    for w in range(2):
        F[w, VX, 0] = zero_layer
        F[w, VY, xr + 1] = zero_layer
        F[w, VZ, xr + 1] = zero_layer
        for i in range(3):
            for t in range(STEPS):
                up_got[t, w, i] = zero_layer
                dn_got[t, w, i] = zero_layer

    def shot_id(index):
        return {"shot": index}

    def slab_id(index):
        return {"slab": index}

    MESH = pl.DeviceIdType.MESH
    barrier = pltpu.get_barrier_semaphore()

    def greet(cond, device):
        @pl.when(cond)
        def _():
            pl.semaphore_signal(barrier, inc=1, device_id=device, device_id_type=MESH)

    has_r = hi < L - 1
    has_l = hi > 0
    has_up = slab < slabs - 1
    has_dn = slab > 0
    pl.semaphore_signal(barrier, inc=1, device_id=shot_id(partner), device_id_type=MESH)
    greet(has_r, shot_id(me + 2))
    greet(has_l, shot_id(me - 2))
    greet(has_up, slab_id(slab + 1))
    greet(has_dn, slab_id(slab - 1))
    one = jnp.int32(1)
    nul = jnp.int32(0)
    count = (
        one
        + jnp.where(has_r, one, nul)
        + jnp.where(has_l, one, nul)
        + jnp.where(has_up, one, nul)
        + jnp.where(has_dn, one, nul)
    )
    pl.semaphore_wait(barrier, count)

    def remote(src, dst, ss, rs, device):
        return pltpu.make_async_remote_copy(
            src_ref=src,
            dst_ref=dst,
            send_sem=ss,
            recv_sem=rs,
            device_id=device,
            device_id_type=MESH,
        )

    def when(cond, fn):
        pl.when(cond)(fn)

    def to_partner(block, src):
        return remote(
            src, slots.at[block], ag_send_y.at[block // 2], ag_recv.at[block], shot_id(partner)
        )

    def to_line(block, src, by, sem):
        return remote(src, slots.at[block], sem, ag_recv.at[block], shot_id(me + 2 * by))

    own_r = to_line(me, mats_in, 1, ag_send_z.at[me])
    own_l = to_line(me, mats_in, -1, ag_send_o.at[0])
    own_p = to_partner(me, mats_in)
    when(has_r, own_r.start)
    when(has_l, own_l.start)
    own_p.start()

    def halo(kind, t):
        if kind == 0:
            up_src, up_dst = up_out.at[t], up_got.at[t]
            dn_src, dn_dst = dn_out.at[t], dn_got.at[t]
        elif kind == 1:
            up_src, up_dst = F.at[:, VX, xr], F.at[:, VX, 0]
            dn_src, dn_dst = F.at[:, pl.ds(VY, 2), 1], F.at[:, pl.ds(VY, 2), xr + 1]
        else:
            up_src, up_dst = mat.at[0, xr], mat.at[0, 0]
            dn_src, dn_dst = mat.at[0, 1], mat.at[0, xr + 1]
        up = remote(
            up_src, up_dst, halo_send.at[0, kind, t], halo_recv.at[0, kind, t], slab_id(slab + 1)
        )
        dn = remote(
            dn_src, dn_dst, halo_send.at[1, kind, t], halo_recv.at[1, kind, t], slab_id(slab - 1)
        )
        return up, dn

    def halo_start(kind, t):
        up, dn = halo(kind, t)
        when(has_up, up.start)
        when(has_dn, dn.start)

    def halo_wait(kind, t):
        up, dn = halo(kind, t)
        when(has_dn, up.wait_recv)
        when(has_up, dn.wait_recv)

    def halo_sent(kind, t):
        up, dn = halo(kind, t)
        when(has_up, up.wait_send)
        when(has_dn, dn.wait_send)

    for c in loads + small:
        c.wait()
    halo_start(1, 0)

    lane = lax.broadcasted_iota(jnp.int32, (ny, nz), 1)
    row = lax.broadcasted_iota(jnp.int32, (ny, nz), 0)

    def up_y(a):
        return jnp.where(row == ny - 1, 0.0, pltpu.roll(a, ny - 1, 0)) - a

    def down_y(a):
        return a - jnp.where(row == 0, 0.0, pltpu.roll(a, 1, 0))

    def up_z(a):
        return jnp.where(lane == nz - 1, 0.0, pltpu.roll(a, nz - 1, 1)) - a

    def down_z(a):
        return a - jnp.where(lane == 0, 0.0, pltpu.roll(a, 1, 1))

    def pack(t):
        for w in range(2):
            sxy, sxz = F[w, SXY, xr], F[w, SXZ, xr]
            up_out[t, w, 0] = down_y(sxy) + down_z(sxz) - F[w, SXX, xr]
            up_out[t, w, 1] = sxz
            up_out[t, w, 2] = sxy
            syz = F[w, SYZ, 1]
            dn_out[t, w, 0] = F[w, SXY, 1] + up_y(F[w, SYY, 1]) + down_z(syz)
            dn_out[t, w, 1] = F[w, SXZ, 1] + down_y(syz) + up_z(F[w, SZZ, 1])
            dn_out[t, w, 2] = F[w, SXX, 1]
        halo_start(0, t)

    def unpack(t):
        halo_wait(0, t)
        for w in range(2):
            F[w, SXZ, 0] = up_got[t, w, 1]
            F[w, SXY, 0] = up_got[t, w, 2]
            F[w, SXX, xr + 1] = dn_got[t, w, 2]

    def ghosts(t):
        for w in range(2):
            F[w, VX, 0] += mat[0, 0] * (F[w, SXX, 1] + up_got[t, w, 0])
            F[w, VY, xr + 1] += mat[0, xr + 1] * (dn_got[t, w, 0] - F[w, SXY, xr])
            F[w, VZ, xr + 1] += mat[0, xr + 1] * (dn_got[t, w, 1] - F[w, SXZ, xr])

    pack(0)

    eye = lax.broadcasted_iota(jnp.int32, (ny, ny), 0) == lax.broadcasted_iota(
        jnp.int32, (ny, ny), 1
    )

    def column(r):
        wide = jnp.broadcast_to(r, (ny, ny))
        return jnp.sum(jnp.where(eye, wide, 0.0), axis=1, keepdims=True)

    def prepare(x, carry):
        cell = ((slab * xr + x) * ny + row) * nz + lane
        total = jnp.zeros((ny, nz), jnp.float32)
        for j in range(cells.shape[1]):
            sign = (2 * encoding[0, j] - 1).astype(jnp.float32)
            total = total + jnp.where(cell == cells[0, j], sign, 0.0)
        image[x] = total
        hit = lane.astype(jnp.float32) == column(depth[pl.ds(x, 1), :].astype(jnp.float32))
        for t in range(STEPS):
            inj[t, x] = jnp.where(hit, column(data[0, t, pl.ds(x, 1), :]), 0.0)
        return carry

    lax.fori_loop(0, xr, prepare, 0)

    for k in range(1, L):
        def right_moving(k=k):
            b = me - 2 * k
            ref = slots.at[b]
            to_line(b, ref, 1, ag_send_z.at[b]).wait_recv()
            when(has_r, to_line(b, ref, 1, ag_send_z.at[b]).start)
            to_partner(b, ref).start()

        def left_moving(k=k):
            b = me + 2 * k
            ref = slots.at[b]
            to_line(b, ref, -1, ag_send_z.at[b]).wait_recv()
            when(has_l, to_line(b, ref, -1, ag_send_z.at[b]).start)
            to_partner(b, ref).start()

        when(hi >= k, right_moving)
        when(hi + k < L, left_moving)
    for h in range(L):
        b = h * 2 + 1 - lo
        to_partner(b, slots.at[b]).wait_recv()

    def assemble(x, carry):
        for c in range(nc):
            whole = jnp.concatenate([slots[i, c, x] for i in range(n)], axis=0)
            mat[c, x + 1] = whole * STEP_SIZE
        return carry

    lax.fori_loop(0, xr, assemble, 0)
    halo_start(2, 0)

    def velocity_layer(t, x):
        forces = []
        old = []
        for w in range(2):
            sxx, sxy, sxz = F[w, SXX, x], F[w, SXY, x], F[w, SXZ, x]
            syz = F[w, SYZ, x]
            fx = (F[w, SXX, x + 1] - sxx) + down_y(sxy) + down_z(sxz)
            fy = (sxy - F[w, SXY, x - 1]) + up_y(F[w, SYY, x]) + down_z(syz)
            fz = (sxz - F[w, SXZ, x - 1]) + down_y(syz) + up_z(F[w, SZZ, x])
            forces.append([fx, fy, fz])
            old.append([F[w, VX, x], F[w, VY, x], F[w, VZ, x]])
        term = (
            forces[0][0] * old[1][0] + forces[0][1] * old[1][1] + forces[0][2] * old[1][2]
        )
        acc[0, x] = term if t == 0 else acc[0, x] + term
        buoy = mat[0, x]
        for w in range(2):
            for c in range(3):
                F[w, c, x] = old[w][c] + buoy * forces[w][c]

    def strain_of(w, x):
        vx, vy, vz = F[w, VX, x], F[w, VY, x], F[w, VZ, x]
        return [
            vx - F[w, VX, x - 1],
            down_y(vy),
            down_z(vz),
            up_z(vy) + up_y(vz),
            up_z(vx) + (F[w, VZ, x + 1] - vz),
            up_y(vx) + (F[w, VY, x + 1] - vy),
        ]

    def add_terms(t, x, f, a, last):
        for i, (p, q) in enumerate(PAIRS):
            term = f[p] * a[q]
            if p != q:
                term = term + f[q] * a[p]
            if t > 0:
                term = term + acc[i + 1, x]
            if last:
                put_block(i + 1, x, term)
            else:
                acc[i + 1, x] = term

    def put_block(c, x, total):
        total = total * scale
        for i in range(n):
            blocks[i, c, x - 1] = total[i * yb : (i + 1) * yb]

    def stress_layer(t, x, strains):
        m = [mat[c, x] for c in range(nc)]
        for w in range(2):
            exx, eyy, ezz, gyz, gxz, gxy = strains[w]
            F[w, SXX, x] = F[w, SXX, x] + (m[1] * exx + m[2] * eyy + m[3] * ezz)
            F[w, SYY, x] = F[w, SYY, x] + (m[2] * exx + m[4] * eyy + m[5] * ezz)
            extra = wavelet[t] * image[x - 1] if w == 0 else inj[t, x - 1]
            F[w, SZZ, x] = F[w, SZZ, x] + (m[3] * exx + m[5] * eyy + m[6] * ezz) + extra
            F[w, SYZ, x] = F[w, SYZ, x] + m[7] * gyz
            F[w, SXZ, x] = F[w, SXZ, x] + m[8] * gxz
            F[w, SXY, x] = F[w, SXY, x] + m[9] * gxy

    def over(start, stop, step, fn):
        def one_layer(j, carry):
            fn(start + j * step)
            return carry

        lax.fori_loop(0, (stop - start + step - 1) // step, one_layer, 0)

    def interior(fn):
        over(2, xr, 1, fn)

    def rims(fn):
        over(1, xr + 1, xr - 1, fn)

    stores = []

    def store(first, count, sem):
        for w, out in ((0, fwd_out), (1, adj_out)):
            c = pltpu.make_async_copy(
                F.at[w, pl.ds(first, count), pl.ds(1, xr)],
                out.at[0, pl.ds(first, count)],
                store_sem.at[sem, w],
            )
            c.start()
            stores.append(c)

    for t in range(STEPS):
        last = t == STEPS - 1
        interior(functools.partial(velocity_layer, t))
        unpack(t)
        if t == 0:
            halo_sent(1, 0)
        rims(functools.partial(velocity_layer, t))
        if t == 0:
            halo_wait(1, 0)
            halo_wait(2, 0)
        ghosts(t)

        def both(x, t=t, last=last):
            strains = [strain_of(w, x) for w in range(2)]
            add_terms(t, x, strains[0], strains[1], last)
            if not last:
                stress_layer(t, x, strains)

        rims(both)
        if not last:
            pack(t + 1)
        interior(both)
    store(0, 3, 0)
    over(1, xr + 1, 1, lambda x: put_block(0, x, acc[0, x]))

    def rs_y(d):
        return remote(
            blocks.at[d * 2 + 1 - lo],
            ry.at[d],
            rs_send_y.at[d],
            rs_recv_y.at[d],
            shot_id(partner),
        )

    def rs_r(d):
        return remote(
            ry.at[d], rright.at[d], rs_send_r.at[d], rs_recv_r.at[d], shot_id(me + 2)
        )

    def rs_l(d):
        return remote(ry.at[d], rleft.at[d], rs_send_l.at[d], rs_recv_l.at[d], shot_id(me - 2))

    for k in range(L - 1, 0, -1):
        when(hi + k < L, lambda k=k: rs_y(hi + k).start())
        when(hi >= k, lambda k=k: rs_y(hi - k).start())
    rs_y(hi).start()

    over(1, xr + 1, 1, lambda x: stress_layer(STEPS - 1, x, [strain_of(w, x) for w in range(2)]))
    store(3, comps - 3, 1)

    def add_into(d, extra):
        def one_layer(x, carry):
            for c in range(nc):
                total = ry[d, c, x] + blocks[d * 2 + lo, c, x]
                if extra is not None:
                    total = total + extra[d, c, x]
                ry[d, c, x] = total
            return carry

        lax.fori_loop(0, xr, one_layer, 0)

    for k in range(L - 1, 0, -1):
        def send_right(k=k):
            d = hi + k
            rs_y(d).wait_recv()

            def plus():
                rs_r(d).wait_recv()
                add_into(d, rright)

            when(has_l, plus)
            when(hi == 0, lambda: add_into(d, None))
            rs_r(d).start()

        def send_left(k=k):
            d = hi - k
            rs_y(d).wait_recv()

            def plus():
                rs_l(d).wait_recv()
                add_into(d, rleft)

            when(has_r, plus)
            when(hi == L - 1, lambda: add_into(d, None))
            rs_l(d).start()

        when(hi + k < L, send_right)
        when(hi >= k, send_left)

    rs_y(hi).wait_recv()
    add_into(hi, None)

    def take(ref):
        def one_layer(x, carry):
            for c in range(nc):
                ry[hi, c, x] = ry[hi, c, x] + ref[hi, c, x]
            return carry

        lax.fori_loop(0, xr, one_layer, 0)

    def from_left():
        rs_r(hi).wait_recv()
        take(rright)

    def from_right():
        rs_l(hi).wait_recv()
        take(rleft)

    when(has_l, from_left)
    when(has_r, from_right)
    final = pltpu.make_async_copy(ry.at[hi], grad_out, load_sem.at[2])
    final.start()

    when(has_r, own_r.wait_send)
    when(has_l, own_l.wait_send)
    own_p.wait_send()
    for k in range(1, L):
        def right_sent(k=k):
            b = me - 2 * k
            when(has_r, to_line(b, slots.at[b], 1, ag_send_z.at[b]).wait_send)
            to_partner(b, slots.at[b]).wait_send()

        def left_sent(k=k):
            b = me + 2 * k
            when(has_l, to_line(b, slots.at[b], -1, ag_send_z.at[b]).wait_send)
            to_partner(b, slots.at[b]).wait_send()

        when(hi >= k, right_sent)
        when(hi + k < L, left_sent)
        when(hi + k < L, lambda k=k: rs_y(hi + k).wait_send())
        when(hi >= k, lambda k=k: rs_y(hi - k).wait_send())
        when(hi + k < L, lambda k=k: rs_r(hi + k).wait_send())
        when(hi >= k, lambda k=k: rs_l(hi - k).wait_send())
    rs_y(hi).wait_send()
    for t in range(STEPS):
        halo_sent(0, t)
    halo_sent(2, 0)
    for c in stores:
        c.wait()
    final.wait()


def solution(mesh):
    n = mesh.shape["shot"]
    slabs = mesh.shape["slab"]

    def body(fwd, adj, mats, wavelet, encoding, cells, depth, data):
        shots, comps, xr, ny, nz = fwd.shape
        nc, _, yb, _ = mats.shape
        L = n // 2
        scale = float(shots * n * STEPS) ** (-0.5)
        any_spec = pl.BlockSpec(memory_space=pl.ANY)
        dma = pltpu.SemaphoreType.DMA
        f32 = jnp.float32
        return pl.pallas_call(
            functools.partial(kernel, n, slabs, scale),
            out_shape=(
                jax.ShapeDtypeStruct(fwd.shape, f32),
                jax.ShapeDtypeStruct(adj.shape, f32),
                jax.ShapeDtypeStruct(mats.shape, f32),
            ),
            in_specs=[any_spec] * 8,
            out_specs=(any_spec, any_spec, any_spec),
            scratch_shapes=[
                pltpu.SMEM(wavelet.shape, f32),
                pltpu.SMEM(encoding.shape, jnp.int32),
                pltpu.SMEM(cells.shape, jnp.int32),
                pltpu.VMEM(depth.shape, jnp.int32),
                pltpu.VMEM(data.shape, f32),
                pltpu.VMEM((2, comps, xr + 2, ny, nz), f32),
                pltpu.VMEM((STEPS, 2, 3, ny, nz), f32),
                pltpu.VMEM((STEPS, 2, 3, ny, nz), f32),
                pltpu.VMEM((STEPS, 2, 3, ny, nz), f32),
                pltpu.VMEM((STEPS, 2, 3, ny, nz), f32),
                pltpu.VMEM((n, nc, xr, yb, nz), f32),
                pltpu.VMEM((nc, xr + 2, ny, nz), f32),
                pltpu.VMEM((nc, xr + 2, ny, nz), f32),
                pltpu.VMEM((xr, ny, nz), f32),
                pltpu.VMEM((STEPS, xr, ny, nz), f32),
                pltpu.VMEM((n, nc, xr, yb, nz), f32),
                pltpu.VMEM((L, nc, xr, yb, nz), f32),
                pltpu.VMEM((L, nc, xr, yb, nz), f32),
                pltpu.VMEM((L, nc, xr, yb, nz), f32),
                dma((8,)),
                dma((2, 2)),
                dma((2, 3, STEPS)),
                dma((2, 3, STEPS)),
                dma((n,)),
                dma((n,)),
                dma((1,)),
                dma((L,)),
                dma((L,)),
                dma((L,)),
                dma((L,)),
                dma((L,)),
                dma((L,)),
                dma((L,)),
            ],
            compiler_params=pltpu.CompilerParams(
                collective_id=0, has_side_effects=True, vmem_limit_bytes=60 * 1024 * 1024
            ),
        )(wavelet, encoding, cells, depth, data, fwd, adj, mats)

    return jax.shard_map(
        body,
        mesh=mesh,
        in_specs=(
            P("shot", None, "slab", None, None),
            P("shot", None, "slab", None, None),
            P(None, "slab", "shot", None),
            P(),
            P("shot", None),
            P("shot", None),
            P("slab", None),
            P("shot", None, "slab", None),
        ),
        out_specs=(
            P("shot", None, "slab", None, None),
            P("shot", None, "slab", None, None),
            P(None, "slab", "shot", None),
        ),
        check_vma=False,
    )
```

```python
import functools

import jax
import jax.numpy as jnp
from jax import lax
from jax.experimental import pallas as pl
from jax.experimental.pallas import tpu as pltpu
from jax.sharding import PartitionSpec as P

STEPS = 4
STEP_SIZE = 0.25
VX, VY, VZ, SXX, SYY, SZZ, SYZ, SXZ, SXY = range(9)
PAIRS = [(0, 0), (0, 1), (0, 2), (1, 1), (1, 2), (2, 2), (3, 3), (4, 4), (5, 5)]


def kernel(
    n,
    slabs,
    scale,
    wavelet_in,
    encoding_in,
    cells_in,
    depth_in,
    data_in,
    fwd_in,
    adj_in,
    mats_in,
    F,
    grad_out,
    wavelet,
    encoding,
    cells,
    depth,
    data,
    up_out,
    dn_out,
    up_got,
    dn_got,
    slots,
    mat,
    acc,
    image,
    inj,
    blocks,
    ry,
    rright,
    rleft,
    load_sem,
    halo_send,
    halo_recv,
    ag_recv,
    ag_send_z,
    ag_send_o,
    ag_send_y,
    rs_recv_y,
    rs_send_y,
    rs_recv_r,
    rs_send_r,
    rs_recv_l,
    rs_send_l,
):
    _, comps, xr, ny, nz = fwd_in.shape
    tiles, rows, _ = mats_in.shape
    nc = mat.shape[0]
    yb = ny // n
    group = rows // yb
    L = n // 2
    me = lax.axis_index("shot")
    slab = lax.axis_index("slab")
    lo = lax.rem(me, 2)
    hi = me // 2
    partner = hi * 2 + 1 - lo

    small = [
        pltpu.make_async_copy(src, dst, load_sem.at[3 + i])
        for i, (src, dst) in enumerate(
            [
                (wavelet_in, wavelet),
                (encoding_in, encoding),
                (cells_in, cells),
                (depth_in, depth),
                (data_in, data),
            ]
        )
    ]
    loads = [
        pltpu.make_async_copy(fwd_in.at[0], F.at[0, :, pl.ds(1, xr)], load_sem.at[0]),
        pltpu.make_async_copy(adj_in.at[0], F.at[1, :, pl.ds(1, xr)], load_sem.at[1]),
        pltpu.make_async_copy(mats_in, slots.at[me], load_sem.at[2]),
    ]
    for c in loads + small:
        c.start()
    zero_layer = jnp.zeros((ny, nz), jnp.float32)
    mat[0, 0] = zero_layer
    mat[0, xr + 1] = zero_layer
    for w in range(2):
        F[w, VX, 0] = zero_layer
        F[w, VY, xr + 1] = zero_layer
        F[w, VZ, xr + 1] = zero_layer
        for i in range(3):
            for t in range(STEPS):
                up_got[t, w, i] = zero_layer
                dn_got[t, w, i] = zero_layer

    def shot_id(index):
        return {"shot": index}

    def slab_id(index):
        return {"slab": index}

    MESH = pl.DeviceIdType.MESH
    barrier = pltpu.get_barrier_semaphore()

    def greet(cond, device):
        @pl.when(cond)
        def _():
            pl.semaphore_signal(barrier, inc=1, device_id=device, device_id_type=MESH)

    has_r = hi < L - 1
    has_l = hi > 0
    has_up = slab < slabs - 1
    has_dn = slab > 0
    pl.semaphore_signal(barrier, inc=1, device_id=shot_id(partner), device_id_type=MESH)
    greet(has_r, shot_id(me + 2))
    greet(has_l, shot_id(me - 2))
    greet(has_up, slab_id(slab + 1))
    greet(has_dn, slab_id(slab - 1))
    one = jnp.int32(1)
    nul = jnp.int32(0)
    count = (
        one
        + jnp.where(has_r, one, nul)
        + jnp.where(has_l, one, nul)
        + jnp.where(has_up, one, nul)
        + jnp.where(has_dn, one, nul)
    )
    pl.semaphore_wait(barrier, count)

    def remote(src, dst, ss, rs, device):
        return pltpu.make_async_remote_copy(
            src_ref=src,
            dst_ref=dst,
            send_sem=ss,
            recv_sem=rs,
            device_id=device,
            device_id_type=MESH,
        )

    def when(cond, fn):
        pl.when(cond)(fn)

    def to_partner(block, src):
        return remote(
            src, slots.at[block], ag_send_y.at[block // 2], ag_recv.at[block], shot_id(partner)
        )

    def to_line(block, src, by, sem):
        return remote(src, slots.at[block], sem, ag_recv.at[block], shot_id(me + 2 * by))

    own_r = to_line(me, mats_in, 1, ag_send_z.at[me])
    own_l = to_line(me, mats_in, -1, ag_send_o.at[0])
    own_p = to_partner(me, mats_in)
    when(has_r, own_r.start)
    when(has_l, own_l.start)
    own_p.start()

    def halo(kind, t):
        if kind == 0:
            up_src, up_dst = up_out.at[t], up_got.at[t]
            dn_src, dn_dst = dn_out.at[t], dn_got.at[t]
        elif kind == 1:
            up_src, up_dst = F.at[:, VX, xr], F.at[:, VX, 0]
            dn_src, dn_dst = F.at[:, pl.ds(VY, 2), 1], F.at[:, pl.ds(VY, 2), xr + 1]
        else:
            up_src, up_dst = mat.at[0, xr], mat.at[0, 0]
            dn_src, dn_dst = mat.at[0, 1], mat.at[0, xr + 1]
        up = remote(
            up_src, up_dst, halo_send.at[0, kind, t], halo_recv.at[0, kind, t], slab_id(slab + 1)
        )
        dn = remote(
            dn_src, dn_dst, halo_send.at[1, kind, t], halo_recv.at[1, kind, t], slab_id(slab - 1)
        )
        return up, dn

    def halo_start(kind, t):
        up, dn = halo(kind, t)
        when(has_up, up.start)
        when(has_dn, dn.start)

    def halo_wait(kind, t):
        up, dn = halo(kind, t)
        when(has_dn, up.wait_recv)
        when(has_up, dn.wait_recv)

    def halo_sent(kind, t):
        up, dn = halo(kind, t)
        when(has_up, up.wait_send)
        when(has_dn, dn.wait_send)

    for c in loads + small:
        c.wait()
    halo_start(1, 0)

    lane = lax.broadcasted_iota(jnp.int32, (ny, nz), 1)
    row = lax.broadcasted_iota(jnp.int32, (ny, nz), 0)

    def up_y(a):
        return jnp.where(row == ny - 1, 0.0, pltpu.roll(a, ny - 1, 0)) - a

    def down_y(a):
        return a - jnp.where(row == 0, 0.0, pltpu.roll(a, 1, 0))

    def up_z(a):
        return jnp.where(lane == nz - 1, 0.0, pltpu.roll(a, nz - 1, 1)) - a

    def down_z(a):
        return a - jnp.where(lane == 0, 0.0, pltpu.roll(a, 1, 1))

    def pack(t):
        for w in range(2):
            sxy, sxz = F[w, SXY, xr], F[w, SXZ, xr]
            up_out[t, w, 0] = down_y(sxy) + down_z(sxz) - F[w, SXX, xr]
            up_out[t, w, 1] = sxz
            up_out[t, w, 2] = sxy
            syz = F[w, SYZ, 1]
            dn_out[t, w, 0] = F[w, SXY, 1] + up_y(F[w, SYY, 1]) + down_z(syz)
            dn_out[t, w, 1] = F[w, SXZ, 1] + down_y(syz) + up_z(F[w, SZZ, 1])
            dn_out[t, w, 2] = F[w, SXX, 1]
        halo_start(0, t)

    def unpack(t):
        halo_wait(0, t)
        for w in range(2):
            F[w, SXZ, 0] = up_got[t, w, 1]
            F[w, SXY, 0] = up_got[t, w, 2]
            F[w, SXX, xr + 1] = dn_got[t, w, 2]

    def ghosts(t):
        for w in range(2):
            F[w, VX, 0] += mat[0, 0] * (F[w, SXX, 1] + up_got[t, w, 0])
            F[w, VY, xr + 1] += mat[0, xr + 1] * (dn_got[t, w, 0] - F[w, SXY, xr])
            F[w, VZ, xr + 1] += mat[0, xr + 1] * (dn_got[t, w, 1] - F[w, SXZ, xr])

    pack(0)

    eye = lax.broadcasted_iota(jnp.int32, (ny, ny), 0) == lax.broadcasted_iota(
        jnp.int32, (ny, ny), 1
    )

    def column(r):
        wide = jnp.broadcast_to(r, (ny, ny))
        return jnp.sum(jnp.where(eye, wide, 0.0), axis=1, keepdims=True)

    def prepare(x, carry):
        cell = ((slab * xr + x) * ny + row) * nz + lane
        total = jnp.zeros((ny, nz), jnp.float32)
        for j in range(cells.shape[1]):
            sign = (2 * encoding[0, j] - 1).astype(jnp.float32)
            total = total + jnp.where(cell == cells[0, j], sign, 0.0)
        image[x] = total
        hit = lane.astype(jnp.float32) == column(depth[pl.ds(x, 1), :].astype(jnp.float32))
        for t in range(STEPS):
            inj[t, x] = jnp.where(hit, column(data[0, t, pl.ds(x, 1), :]), 0.0)
        return carry

    lax.fori_loop(0, xr, prepare, 0)

    for k in range(1, L):
        def right_moving(k=k):
            b = me - 2 * k
            ref = slots.at[b]
            to_line(b, ref, 1, ag_send_z.at[b]).wait_recv()
            when(has_r, to_line(b, ref, 1, ag_send_z.at[b]).start)
            to_partner(b, ref).start()

        def left_moving(k=k):
            b = me + 2 * k
            ref = slots.at[b]
            to_line(b, ref, -1, ag_send_z.at[b]).wait_recv()
            when(has_l, to_line(b, ref, -1, ag_send_z.at[b]).start)
            to_partner(b, ref).start()

        when(hi >= k, right_moving)
        when(hi + k < L, left_moving)
    for h in range(L):
        b = h * 2 + 1 - lo
        to_partner(b, slots.at[b]).wait_recv()

    def assemble(xg, carry):
        for c in range(nc):
            held = [slots[i, c * (xr // group) + xg] for i in range(n)]
            for j in range(group):
                whole = jnp.concatenate([h[j * yb : (j + 1) * yb] for h in held], axis=0)
                mat[c, xg * group + j + 1] = whole * STEP_SIZE
        return carry

    lax.fori_loop(0, xr // group, assemble, 0)
    halo_start(2, 0)

    def velocity_layer(t, x):
        forces = []
        old = []
        for w in range(2):
            sxx, sxy, sxz = F[w, SXX, x], F[w, SXY, x], F[w, SXZ, x]
            syz = F[w, SYZ, x]
            fx = (F[w, SXX, x + 1] - sxx) + down_y(sxy) + down_z(sxz)
            fy = (sxy - F[w, SXY, x - 1]) + up_y(F[w, SYY, x]) + down_z(syz)
            fz = (sxz - F[w, SXZ, x - 1]) + down_y(syz) + up_z(F[w, SZZ, x])
            forces.append([fx, fy, fz])
            old.append([F[w, VX, x], F[w, VY, x], F[w, VZ, x]])
        term = (
            forces[0][0] * old[1][0] + forces[0][1] * old[1][1] + forces[0][2] * old[1][2]
        )
        acc[0, x] = term if t == 0 else acc[0, x] + term
        buoy = mat[0, x]
        for w in range(2):
            for c in range(3):
                F[w, c, x] = old[w][c] + buoy * forces[w][c]

    def strain_of(w, x):
        vx, vy, vz = F[w, VX, x], F[w, VY, x], F[w, VZ, x]
        return [
            vx - F[w, VX, x - 1],
            down_y(vy),
            down_z(vz),
            up_z(vy) + up_y(vz),
            up_z(vx) + (F[w, VZ, x + 1] - vz),
            up_y(vx) + (F[w, VY, x + 1] - vy),
        ]

    def add_terms(t, x, f, a):
        for i, (p, q) in enumerate(PAIRS):
            term = f[p] * a[q]
            if p != q:
                term = term + f[q] * a[p]
            if t > 0:
                term = term + acc[i + 1, x]
            acc[i + 1, x] = term

    def put_blocks(xg):
        for c in range(nc):
            held = [acc[c, xg * group + j + 1] * scale for j in range(group)]
            for i in range(n):
                blocks[i, c * (xr // group) + xg] = jnp.concatenate(
                    [h[i * yb : (i + 1) * yb] for h in held], axis=0
                )

    def stress_layer(t, x, strains):
        m = [mat[c, x] for c in range(nc)]
        for w in range(2):
            exx, eyy, ezz, gyz, gxz, gxy = strains[w]
            F[w, SXX, x] = F[w, SXX, x] + (m[1] * exx + m[2] * eyy + m[3] * ezz)
            F[w, SYY, x] = F[w, SYY, x] + (m[2] * exx + m[4] * eyy + m[5] * ezz)
            extra = wavelet[t] * image[x - 1] if w == 0 else inj[t, x - 1]
            F[w, SZZ, x] = F[w, SZZ, x] + (m[3] * exx + m[5] * eyy + m[6] * ezz) + extra
            F[w, SYZ, x] = F[w, SYZ, x] + m[7] * gyz
            F[w, SXZ, x] = F[w, SXZ, x] + m[8] * gxz
            F[w, SXY, x] = F[w, SXY, x] + m[9] * gxy

    def over(start, stop, step, fn):
        def one_layer(j, carry):
            fn(start + j * step)
            return carry

        lax.fori_loop(0, (stop - start + step - 1) // step, one_layer, 0)

    def interior(fn):
        over(2, xr, 1, fn)

    def rims(fn):
        over(1, xr + 1, xr - 1, fn)

    for t in range(STEPS):
        last = t == STEPS - 1
        interior(functools.partial(velocity_layer, t))
        unpack(t)
        if t == 0:
            halo_sent(1, 0)
        rims(functools.partial(velocity_layer, t))
        if t == 0:
            halo_wait(1, 0)
            halo_wait(2, 0)
        ghosts(t)

        def both(x, t=t, last=last):
            strains = [strain_of(w, x) for w in range(2)]
            add_terms(t, x, strains[0], strains[1])
            if not last:
                stress_layer(t, x, strains)

        rims(both)
        if not last:
            pack(t + 1)
        interior(both)
    over(0, xr // group, 1, put_blocks)

    def rs_y(d):
        return remote(
            blocks.at[d * 2 + 1 - lo],
            ry.at[d],
            rs_send_y.at[d],
            rs_recv_y.at[d],
            shot_id(partner),
        )

    def rs_r(d):
        return remote(
            ry.at[d], rright.at[d], rs_send_r.at[d], rs_recv_r.at[d], shot_id(me + 2)
        )

    def rs_l(d):
        return remote(ry.at[d], rleft.at[d], rs_send_l.at[d], rs_recv_l.at[d], shot_id(me - 2))

    for k in range(L - 1, 0, -1):
        when(hi + k < L, lambda k=k: rs_y(hi + k).start())
        when(hi >= k, lambda k=k: rs_y(hi - k).start())
    rs_y(hi).start()

    over(1, xr + 1, 1, lambda x: stress_layer(STEPS - 1, x, [strain_of(w, x) for w in range(2)]))

    def add_into(d, extra, target):
        def one_layer(x, carry):
            for c in range(nc):
                i = x * nc + c
                total = ry[d, i] + blocks[d * 2 + lo, i]
                if extra is not None:
                    total = total + extra[d, i]
                target[i] = total
            return carry

        lax.fori_loop(0, tiles // nc, one_layer, 0)

    for k in range(L - 1, 0, -1):
        def send_right(k=k):
            d = hi + k
            rs_y(d).wait_recv()

            def plus():
                rs_r(d).wait_recv()
                add_into(d, rright, ry.at[d])

            when(has_l, plus)
            when(hi == 0, lambda: add_into(d, None, ry.at[d]))
            rs_r(d).start()

        def send_left(k=k):
            d = hi - k
            rs_y(d).wait_recv()

            def plus():
                rs_l(d).wait_recv()
                add_into(d, rleft, ry.at[d])

            when(has_r, plus)
            when(hi == L - 1, lambda: add_into(d, None, ry.at[d]))
            rs_l(d).start()

        when(hi + k < L, send_right)
        when(hi >= k, send_left)

    rs_y(hi).wait_recv()
    add_into(hi, None, grad_out)

    def take(ref):
        def one_layer(x, carry):
            for c in range(nc):
                i = x * nc + c
                grad_out[i] = grad_out[i] + ref[hi, i]
            return carry

        lax.fori_loop(0, tiles // nc, one_layer, 0)

    def from_left():
        rs_r(hi).wait_recv()
        take(rright)

    def from_right():
        rs_l(hi).wait_recv()
        take(rleft)

    when(has_l, from_left)
    when(has_r, from_right)

    when(has_r, own_r.wait_send)
    when(has_l, own_l.wait_send)
    own_p.wait_send()
    for k in range(1, L):
        def right_sent(k=k):
            b = me - 2 * k
            when(has_r, to_line(b, slots.at[b], 1, ag_send_z.at[b]).wait_send)
            to_partner(b, slots.at[b]).wait_send()

        def left_sent(k=k):
            b = me + 2 * k
            when(has_l, to_line(b, slots.at[b], -1, ag_send_z.at[b]).wait_send)
            to_partner(b, slots.at[b]).wait_send()

        when(hi >= k, right_sent)
        when(hi + k < L, left_sent)
        when(hi + k < L, lambda k=k: rs_y(hi + k).wait_send())
        when(hi >= k, lambda k=k: rs_y(hi - k).wait_send())
        when(hi + k < L, lambda k=k: rs_r(hi + k).wait_send())
        when(hi >= k, lambda k=k: rs_l(hi - k).wait_send())
    rs_y(hi).wait_send()
    for t in range(STEPS):
        halo_sent(0, t)
    halo_sent(2, 0)


def write_out(F, grad, fwd_out, adj_out, grad_out, sem):
    xr = fwd_out.shape[2]
    comps = fwd_out.shape[1]
    half = comps // 2
    copies = [pltpu.make_async_copy(grad, grad_out, sem.at[4])]
    for w, out in ((0, fwd_out), (1, adj_out)):
        for j, (first, count) in enumerate(((0, half), (half, comps - half))):
            copies.append(
                pltpu.make_async_copy(
                    F.at[w, pl.ds(first, count), pl.ds(1, xr)],
                    out.at[0, pl.ds(first, count)],
                    sem.at[2 * w + j],
                )
            )
    for c in copies:
        c.start()
    for c in copies:
        c.wait()


def solution(mesh):
    n = mesh.shape["shot"]
    slabs = mesh.shape["slab"]

    def body(fwd, adj, mats, wavelet, encoding, cells, depth, data):
        shots, comps, xr, ny, nz = fwd.shape
        nc, _, yb, _ = mats.shape
        L = n // 2
        scale = float(shots * n * STEPS) ** (-0.5)
        rows = max(8, yb)
        tiles = nc * xr * yb // rows
        flat = mats.reshape(tiles, rows, nz)
        vmem = pl.BlockSpec(memory_space=pltpu.VMEM)
        hbm = pl.BlockSpec(memory_space=pltpu.HBM)
        any_spec = pl.BlockSpec(memory_space=pl.ANY)
        dma = pltpu.SemaphoreType.DMA
        f32 = jnp.float32
        fields, grad = pl.pallas_call(
            functools.partial(kernel, n, slabs, scale),
            out_shape=(
                pltpu.VMEM((2, comps, xr + 2, ny, nz), f32),
                pltpu.VMEM(flat.shape, f32),
            ),
            in_specs=[any_spec] * 8,
            out_specs=(vmem, vmem),
            scratch_shapes=[
                pltpu.SMEM(wavelet.shape, f32),
                pltpu.SMEM(encoding.shape, jnp.int32),
                pltpu.SMEM(cells.shape, jnp.int32),
                pltpu.VMEM(depth.shape, jnp.int32),
                pltpu.VMEM(data.shape, f32),
                pltpu.VMEM((STEPS, 2, 3, ny, nz), f32),
                pltpu.VMEM((STEPS, 2, 3, ny, nz), f32),
                pltpu.VMEM((STEPS, 2, 3, ny, nz), f32),
                pltpu.VMEM((STEPS, 2, 3, ny, nz), f32),
                pltpu.VMEM((n, tiles, rows, nz), f32),
                pltpu.VMEM((nc, xr + 2, ny, nz), f32),
                pltpu.VMEM((nc, xr + 2, ny, nz), f32),
                pltpu.VMEM((xr, ny, nz), f32),
                pltpu.VMEM((STEPS, xr, ny, nz), f32),
                pltpu.VMEM((n, tiles, rows, nz), f32),
                pltpu.VMEM((L, tiles, rows, nz), f32),
                pltpu.VMEM((L, tiles, rows, nz), f32),
                pltpu.VMEM((L, tiles, rows, nz), f32),
                dma((8,)),
                dma((2, 3, STEPS)),
                dma((2, 3, STEPS)),
                dma((n,)),
                dma((n,)),
                dma((1,)),
                dma((L,)),
                dma((L,)),
                dma((L,)),
                dma((L,)),
                dma((L,)),
                dma((L,)),
                dma((L,)),
            ],
            compiler_params=pltpu.CompilerParams(
                collective_id=0, has_side_effects=True, vmem_limit_bytes=56 * 1024 * 1024
            ),
        )(wavelet, encoding, cells, depth, data, fwd, adj, flat)
        fwd_out, adj_out, grad = pl.pallas_call(
            write_out,
            out_shape=(
                pltpu.HBM(fwd.shape, f32),
                pltpu.HBM(adj.shape, f32),
                pltpu.HBM(flat.shape, f32),
            ),
            in_specs=[vmem, vmem],
            out_specs=(hbm, hbm, hbm),
            scratch_shapes=[dma((5,))],
            compiler_params=pltpu.CompilerParams(vmem_limit_bytes=8 * 1024 * 1024),
        )(fields, grad)
        return fwd_out, adj_out, grad.reshape(mats.shape)

    return jax.shard_map(
        body,
        mesh=mesh,
        in_specs=(
            P("shot", None, "slab", None, None),
            P("shot", None, "slab", None, None),
            P(None, "slab", "shot", None),
            P(),
            P("shot", None),
            P("shot", None),
            P("slab", None),
            P("shot", None, "slab", None),
        ),
        out_specs=(
            P("shot", None, "slab", None, None),
            P("shot", None, "slab", None, None),
            P(None, "slab", "shot", None),
        ),
        check_vma=False,
    )
```

```python
import functools

import jax
import jax.numpy as jnp
from jax import lax
from jax.experimental import pallas as pl
from jax.experimental.pallas import tpu as pltpu
from jax.sharding import PartitionSpec as P

STEPS = 4
STEP_SIZE = 0.25
VX, VY, VZ, SXX, SYY, SZZ, SYZ, SXZ, SXY = range(9)
PAIRS = [(0, 0), (0, 1), (0, 2), (1, 1), (1, 2), (2, 2), (3, 3), (4, 4), (5, 5)]


def kernel(
    n,
    slabs,
    scale,
    wavelet_in,
    encoding_in,
    cells_in,
    depth_in,
    data_in,
    fwd_in,
    adj_in,
    mats_in,
    F,
    grad_out,
    wavelet,
    encoding,
    cells,
    depth,
    data,
    up_out,
    dn_out,
    up_got,
    dn_got,
    slots,
    mat,
    acc,
    image,
    inj,
    blocks,
    ry,
    rright,
    rleft,
    load_sem,
    halo_send,
    halo_recv,
    ag_recv,
    ag_send_z,
    ag_send_o,
    ag_send_y,
    rs_recv_y,
    rs_send_y,
    rs_recv_r,
    rs_send_r,
    rs_recv_l,
    rs_send_l,
):
    _, comps, xr, ny, nz = fwd_in.shape
    tiles, rows, _ = mats_in.shape
    nc = mat.shape[0]
    yb = ny // n
    group = rows // yb
    nh = F.shape[4]
    half = ny // 2
    first = (0, ny - nh)
    early = nh // yb
    L = n // 2
    me = lax.axis_index("shot")
    slab = lax.axis_index("slab")
    lo = lax.rem(me, 2)
    hi = me // 2
    partner = hi * 2 + 1 - lo

    small = [
        pltpu.make_async_copy(src, dst, load_sem.at[3 + i])
        for i, (src, dst) in enumerate(
            [
                (wavelet_in, wavelet),
                (encoding_in, encoding),
                (cells_in, cells),
                (depth_in, depth),
                (data_in, data),
            ]
        )
    ]
    loads = [
        pltpu.make_async_copy(
            src.at[0, :, :, pl.ds(first[s], nh)],
            F.at[s, w, :, pl.ds(1, xr)],
            load_sem.at[8 + 2 * s + w],
        )
        for s in range(2)
        for w, src in ((0, fwd_in), (1, adj_in))
    ]
    loads.append(pltpu.make_async_copy(mats_in, slots.at[me], load_sem.at[2]))
    for c in loads + small:
        c.start()
    mat[0, 0] = jnp.zeros((ny, nz), jnp.float32)
    mat[0, xr + 1] = jnp.zeros((ny, nz), jnp.float32)
    zero_layer = jnp.zeros((nh, nz), jnp.float32)
    for s in range(2):
        for w in range(2):
            F[s, w, VX, 0] = zero_layer
            F[s, w, VY, xr + 1] = zero_layer
            F[s, w, VZ, xr + 1] = zero_layer
            for i in range(3):
                for t in range(STEPS):
                    up_got[s, t, w, i] = zero_layer
                    dn_got[s, t, w, i] = zero_layer

    def shot_id(index):
        return {"shot": index}

    def slab_id(index):
        return {"slab": index}

    MESH = pl.DeviceIdType.MESH
    barrier = pltpu.get_barrier_semaphore()

    def greet(cond, device):
        @pl.when(cond)
        def _():
            pl.semaphore_signal(barrier, inc=1, device_id=device, device_id_type=MESH)

    has_r = hi < L - 1
    has_l = hi > 0
    has_up = slab < slabs - 1
    has_dn = slab > 0
    pl.semaphore_signal(barrier, inc=1, device_id=shot_id(partner), device_id_type=MESH)
    greet(has_r, shot_id(me + 2))
    greet(has_l, shot_id(me - 2))
    greet(has_up, slab_id(slab + 1))
    greet(has_dn, slab_id(slab - 1))
    one = jnp.int32(1)
    nul = jnp.int32(0)
    count = (
        one
        + jnp.where(has_r, one, nul)
        + jnp.where(has_l, one, nul)
        + jnp.where(has_up, one, nul)
        + jnp.where(has_dn, one, nul)
    )
    pl.semaphore_wait(barrier, count)

    def remote(src, dst, ss, rs, device):
        return pltpu.make_async_remote_copy(
            src_ref=src,
            dst_ref=dst,
            send_sem=ss,
            recv_sem=rs,
            device_id=device,
            device_id_type=MESH,
        )

    def when(cond, fn):
        pl.when(cond)(fn)

    def to_partner(block, src):
        return remote(
            src, slots.at[block], ag_send_y.at[block // 2], ag_recv.at[block], shot_id(partner)
        )

    def to_line(block, src, by, sem):
        return remote(src, slots.at[block], sem, ag_recv.at[block], shot_id(me + 2 * by))

    own_r = to_line(me, mats_in, 1, ag_send_z.at[me])
    own_l = to_line(me, mats_in, -1, ag_send_o.at[0])
    own_p = to_partner(me, mats_in)
    when(has_r, own_r.start)
    when(has_l, own_l.start)
    own_p.start()

    def halo(kind, s, t):
        if kind == 0:
            up_src, up_dst = up_out.at[s, t], up_got.at[s, t]
            dn_src, dn_dst = dn_out.at[s, t], dn_got.at[s, t]
        elif kind == 1:
            up_src, up_dst = F.at[s, :, VX, xr], F.at[s, :, VX, 0]
            dn_src, dn_dst = F.at[s, :, pl.ds(VY, 2), 1], F.at[s, :, pl.ds(VY, 2), xr + 1]
        else:
            part = pl.ds(0, nh) if s == 0 else pl.ds(nh, ny - nh)
            up_src, up_dst = mat.at[0, xr, part], mat.at[0, 0, part]
            dn_src, dn_dst = mat.at[0, 1, part], mat.at[0, xr + 1, part]
        i = s * STEPS + t
        up = remote(
            up_src, up_dst, halo_send.at[0, kind, i], halo_recv.at[0, kind, i], slab_id(slab + 1)
        )
        dn = remote(
            dn_src, dn_dst, halo_send.at[1, kind, i], halo_recv.at[1, kind, i], slab_id(slab - 1)
        )
        return up, dn

    def halo_start(kind, s, t):
        up, dn = halo(kind, s, t)
        when(has_up, up.start)
        when(has_dn, dn.start)

    def halo_wait(kind, s, t):
        up, dn = halo(kind, s, t)
        when(has_dn, up.wait_recv)
        when(has_up, dn.wait_recv)

    def halo_sent(kind, s, t):
        up, dn = halo(kind, s, t)
        when(has_up, up.wait_send)
        when(has_dn, dn.wait_send)

    for c in loads + small:
        c.wait()
    for s in range(2):
        halo_start(1, s, 0)

    lane = lax.broadcasted_iota(jnp.int32, (nh, nz), 1)
    row = lax.broadcasted_iota(jnp.int32, (nh, nz), 0)
    wide_lane = lax.broadcasted_iota(jnp.int32, (ny, nz), 1)
    wide_row = lax.broadcasted_iota(jnp.int32, (ny, nz), 0)

    def up_y(a):
        return jnp.where(row == nh - 1, 0.0, pltpu.roll(a, nh - 1, 0)) - a

    def down_y(a):
        return a - jnp.where(row == 0, 0.0, pltpu.roll(a, 1, 0))

    def up_z(a):
        return jnp.where(lane == nz - 1, 0.0, pltpu.roll(a, nz - 1, 1)) - a

    def down_z(a):
        return a - jnp.where(lane == 0, 0.0, pltpu.roll(a, 1, 1))

    def pack(s, t):
        for w in range(2):
            sxy, sxz = F[s, w, SXY, xr], F[s, w, SXZ, xr]
            up_out[s, t, w, 0] = down_y(sxy) + down_z(sxz) - F[s, w, SXX, xr]
            up_out[s, t, w, 1] = sxz
            up_out[s, t, w, 2] = sxy
            syz = F[s, w, SYZ, 1]
            dn_out[s, t, w, 0] = F[s, w, SXY, 1] + up_y(F[s, w, SYY, 1]) + down_z(syz)
            dn_out[s, t, w, 1] = F[s, w, SXZ, 1] + down_y(syz) + up_z(F[s, w, SZZ, 1])
            dn_out[s, t, w, 2] = F[s, w, SXX, 1]
        halo_start(0, s, t)

    def unpack(s, t):
        halo_wait(0, s, t)
        for w in range(2):
            F[s, w, SXZ, 0] = up_got[s, t, w, 1]
            F[s, w, SXY, 0] = up_got[s, t, w, 2]
            F[s, w, SXX, xr + 1] = dn_got[s, t, w, 2]

    def ghosts(s, t):
        part = pl.ds(first[s], nh)
        for w in range(2):
            F[s, w, VX, 0] += mat[0, 0, part] * (F[s, w, SXX, 1] + up_got[s, t, w, 0])
            F[s, w, VY, xr + 1] += mat[0, xr + 1, part] * (dn_got[s, t, w, 0] - F[s, w, SXY, xr])
            F[s, w, VZ, xr + 1] += mat[0, xr + 1, part] * (dn_got[s, t, w, 1] - F[s, w, SXZ, xr])

    for s in range(2):
        pack(s, 0)

    eye = lax.broadcasted_iota(jnp.int32, (ny, ny), 0) == lax.broadcasted_iota(
        jnp.int32, (ny, ny), 1
    )

    def column(r):
        wide = jnp.broadcast_to(r, (ny, ny))
        return jnp.sum(jnp.where(eye, wide, 0.0), axis=1, keepdims=True)

    def prepare(x, carry):
        cell = ((slab * xr + x) * ny + wide_row) * nz + wide_lane
        total = jnp.zeros((ny, nz), jnp.float32)
        for j in range(cells.shape[1]):
            sign = (2 * encoding[0, j] - 1).astype(jnp.float32)
            total = total + jnp.where(cell == cells[0, j], sign, 0.0)
        image[x] = total
        hit = wide_lane.astype(jnp.float32) == column(depth[pl.ds(x, 1), :].astype(jnp.float32))
        for t in range(STEPS):
            inj[t, x] = jnp.where(hit, column(data[0, t, pl.ds(x, 1), :]), 0.0)
        return carry

    lax.fori_loop(0, xr, prepare, 0)

    def arrived(b, by, more):
        ref = slots.at[b]
        to_line(b, ref, by, ag_send_z.at[b]).wait_recv()
        when(more, to_line(b, ref, by, ag_send_z.at[b]).start)
        to_partner(b, ref).start()

    for k in range(1, L):
        when(hi >= k, lambda k=k: arrived(me - 2 * k, 1, has_r))
        when(hi + k < L - 1, lambda k=k: arrived(me + 2 * k, -1, has_l))

    def from_partner(h):
        b = h * 2 + 1 - lo
        to_partner(b, slots.at[b]).wait_recv()

    early_pairs = -(-early // 2)
    for h in range(early_pairs):
        from_partner(h)

    def assemble(s, xg, carry):
        low, high = ((0, early), (early, n))[s]
        for c in range(nc):
            held = [slots[i, c * (xr // group) + xg] for i in range(low, high)]
            for j in range(group):
                whole = jnp.concatenate([h[j * yb : (j + 1) * yb] for h in held], axis=0)
                mat[c, xg * group + j + 1, pl.ds(low * yb, (high - low) * yb)] = (
                    whole * STEP_SIZE
                )
        return carry

    def last_pair():
        when(hi < L - 1, lambda: arrived((L - 1) * 2 + lo, -1, has_l))

    lax.fori_loop(0, xr // group, functools.partial(assemble, 0), 0)
    halo_start(2, 0, 0)

    def velocity_layer(s, t, x):
        forces = []
        old = []
        for w in range(2):
            sxx, sxy, sxz = F[s, w, SXX, x], F[s, w, SXY, x], F[s, w, SXZ, x]
            syz = F[s, w, SYZ, x]
            fx = (F[s, w, SXX, x + 1] - sxx) + down_y(sxy) + down_z(sxz)
            fy = (sxy - F[s, w, SXY, x - 1]) + up_y(F[s, w, SYY, x]) + down_z(syz)
            fz = (sxz - F[s, w, SXZ, x - 1]) + down_y(syz) + up_z(F[s, w, SZZ, x])
            forces.append([fx, fy, fz])
            old.append([F[s, w, VX, x], F[s, w, VY, x], F[s, w, VZ, x]])
        term = (
            forces[0][0] * old[1][0] + forces[0][1] * old[1][1] + forces[0][2] * old[1][2]
        )
        acc[s, 0, x] = term if t == 0 else acc[s, 0, x] + term
        buoy = mat[0, x, pl.ds(first[s], nh)]
        for w in range(2):
            for c in range(3):
                F[s, w, c, x] = old[w][c] + buoy * forces[w][c]

    def strain_of(s, w, x):
        vx, vy, vz = F[s, w, VX, x], F[s, w, VY, x], F[s, w, VZ, x]
        return [
            vx - F[s, w, VX, x - 1],
            down_y(vy),
            down_z(vz),
            up_z(vy) + up_y(vz),
            up_z(vx) + (F[s, w, VZ, x + 1] - vz),
            up_y(vx) + (F[s, w, VY, x + 1] - vy),
        ]

    def add_terms(s, t, x, f, a):
        for i, (p, q) in enumerate(PAIRS):
            term = f[p] * a[q]
            if p != q:
                term = term + f[q] * a[p]
            if t > 0:
                term = term + acc[s, i + 1, x]
            acc[s, i + 1, x] = term

    def put_blocks(s, xg):
        for c in range(nc):
            held = [acc[s, c, xg * group + j + 1] * scale for j in range(group)]
            for i in range(s * n // 2, (s + 1) * n // 2):
                at = i * yb - first[s]
                blocks[i, c * (xr // group) + xg] = jnp.concatenate(
                    [h[at : at + yb] for h in held], axis=0
                )

    def stress_layer(s, t, x, strains):
        m = [mat[c, x, pl.ds(first[s], nh)] for c in range(nc)]
        for w in range(2):
            exx, eyy, ezz, gyz, gxz, gxy = strains[w]
            F[s, w, SXX, x] = F[s, w, SXX, x] + (m[1] * exx + m[2] * eyy + m[3] * ezz)
            F[s, w, SYY, x] = F[s, w, SYY, x] + (m[2] * exx + m[4] * eyy + m[5] * ezz)
            extra = wavelet[t] * image[x - 1, pl.ds(first[s], nh)] if w == 0 else inj[t, x - 1, pl.ds(first[s], nh)]
            F[s, w, SZZ, x] = F[s, w, SZZ, x] + (m[3] * exx + m[5] * eyy + m[6] * ezz) + extra
            F[s, w, SYZ, x] = F[s, w, SYZ, x] + m[7] * gyz
            F[s, w, SXZ, x] = F[s, w, SXZ, x] + m[8] * gxz
            F[s, w, SXY, x] = F[s, w, SXY, x] + m[9] * gxy

    def over(start, stop, step, fn):
        def one_layer(j, carry):
            fn(start + j * step)
            return carry

        lax.fori_loop(0, (stop - start + step - 1) // step, one_layer, 0)

    def interior(fn):
        over(2, xr, 1, fn)

    def rims(fn):
        over(1, xr + 1, xr - 1, fn)

    def run_step(s, t):
        last = t == STEPS - 1
        interior(functools.partial(velocity_layer, s, t))
        unpack(s, t)
        if t == 0:
            halo_sent(1, s, 0)
        rims(functools.partial(velocity_layer, s, t))
        if t == 0:
            halo_wait(1, s, 0)
            halo_wait(2, s, 0)
        ghosts(s, t)

        def both(x):
            strains = [strain_of(s, w, x) for w in range(2)]
            add_terms(s, t, x, strains[0], strains[1])
            if not last:
                stress_layer(s, t, x, strains)

        rims(both)
        if not last:
            pack(s, t + 1)
        interior(both)
        if last:
            over(0, xr // group, 1, functools.partial(put_blocks, s))

    def last_stress(s):
        over(
            1,
            xr + 1,
            1,
            lambda x: stress_layer(s, STEPS - 1, x, [strain_of(s, w, x) for w in range(2)]),
        )

    def rs_y(d):
        return remote(
            blocks.at[d * 2 + 1 - lo],
            ry.at[d],
            rs_send_y.at[d],
            rs_recv_y.at[d],
            shot_id(partner),
        )

    def rs_r(d):
        return remote(
            ry.at[d], rright.at[d], rs_send_r.at[d], rs_recv_r.at[d], shot_id(me + 2)
        )

    def rs_l(d):
        return remote(ry.at[d], rleft.at[d], rs_send_l.at[d], rs_recv_l.at[d], shot_id(me - 2))

    def inside(s, d):
        return (d >= s * L // 2) & (d < (s + 1) * L // 2)

    def scatter_start(s):
        for k in range(L - 1, 0, -1):
            when(inside(s, hi + k), lambda k=k: rs_y(hi + k).start())
            when(inside(s, hi - k), lambda k=k: rs_y(hi - k).start())
        when(inside(s, hi), lambda: rs_y(hi).start())

    def add_into(d, extra, target):
        def one_layer(x, carry):
            for c in range(nc):
                i = x * nc + c
                total = ry[d, i] + blocks[d * 2 + lo, i]
                if extra is not None:
                    total = total + extra[d, i]
                target[i] = total
            return carry

        lax.fori_loop(0, tiles // nc, one_layer, 0)

    def scatter_round(s, k):
        def send_right():
            d = hi + k
            rs_y(d).wait_recv()

            def plus():
                rs_r(d).wait_recv()
                add_into(d, rright, ry.at[d])

            when(has_l, plus)
            when(hi == 0, lambda: add_into(d, None, ry.at[d]))
            rs_r(d).start()

        def send_left():
            d = hi - k
            rs_y(d).wait_recv()

            def plus():
                rs_l(d).wait_recv()
                add_into(d, rleft, ry.at[d])

            when(has_r, plus)
            when(hi == L - 1, lambda: add_into(d, None, ry.at[d]))
            rs_l(d).start()

        when(inside(s, hi + k), send_right)
        when(inside(s, hi - k), send_left)

    run_step(0, 0)
    last_pair()
    run_step(0, 1)
    run_step(0, 2)
    run_step(0, 3)
    scatter_start(0)
    for h in range(early_pairs, L):
        from_partner(h)
    lax.fori_loop(0, xr // group, functools.partial(assemble, 1), 0)
    halo_start(2, 1, 0)
    last_stress(0)
    rounds = [[] for t in range(STEPS)]
    for k in range(L - 1, 0, -1):
        rounds[min(L - k, STEPS - 1)].append(k)
    for t in range(STEPS):
        run_step(1, t)
        if t == STEPS - 1:
            scatter_start(1)
        for k in rounds[t]:
            scatter_round(0, k)
    last_stress(1)
    for k in range(L - 1, 0, -1):
        scatter_round(1, k)

    rs_y(hi).wait_recv()
    add_into(hi, None, grad_out)

    def take(ref):
        def one_layer(x, carry):
            for c in range(nc):
                i = x * nc + c
                grad_out[i] = grad_out[i] + ref[hi, i]
            return carry

        lax.fori_loop(0, tiles // nc, one_layer, 0)

    def from_left():
        rs_r(hi).wait_recv()
        take(rright)

    def from_right():
        rs_l(hi).wait_recv()
        take(rleft)

    when(has_l, from_left)
    when(has_r, from_right)

    when(has_r, own_r.wait_send)
    when(has_l, own_l.wait_send)
    own_p.wait_send()
    for k in range(1, L):
        def right_sent(k=k):
            b = me - 2 * k
            when(has_r, to_line(b, slots.at[b], 1, ag_send_z.at[b]).wait_send)
            to_partner(b, slots.at[b]).wait_send()

        def left_sent(k=k):
            b = me + 2 * k
            when(has_l, to_line(b, slots.at[b], -1, ag_send_z.at[b]).wait_send)
            to_partner(b, slots.at[b]).wait_send()

        when(hi >= k, right_sent)
        when(hi + k < L, left_sent)
        when(hi + k < L, lambda k=k: rs_y(hi + k).wait_send())
        when(hi >= k, lambda k=k: rs_y(hi - k).wait_send())
        when(hi + k < L, lambda k=k: rs_r(hi + k).wait_send())
        when(hi >= k, lambda k=k: rs_l(hi - k).wait_send())
    rs_y(hi).wait_send()
    for s in range(2):
        for t in range(STEPS):
            halo_sent(0, s, t)
        halo_sent(2, s, 0)


def write_out(F, grad, fwd_out, adj_out, grad_out, sem):
    xr, ny = fwd_out.shape[2:4]
    half = ny // 2
    copies = [pltpu.make_async_copy(grad, grad_out, sem.at[4])]
    for w, out in ((0, fwd_out), (1, adj_out)):
        for s, at in ((0, 0), (1, F.shape[4] - half)):
            copies.append(
                pltpu.make_async_copy(
                    F.at[s, w, :, pl.ds(1, xr), pl.ds(at, half)],
                    out.at[0, :, :, pl.ds(s * half, half)],
                    sem.at[2 * w + s],
                )
            )
    for c in copies:
        c.start()
    for c in copies:
        c.wait()


def solution(mesh):
    n = mesh.shape["shot"]
    slabs = mesh.shape["slab"]

    def body(fwd, adj, mats, wavelet, encoding, cells, depth, data):
        shots, comps, xr, ny, nz = fwd.shape
        nc, _, yb, _ = mats.shape
        L = n // 2
        nh = ny // 2 + 2 * STEPS
        scale = float(shots * n * STEPS) ** (-0.5)
        rows = max(8, yb)
        tiles = nc * xr * yb // rows
        flat = mats.reshape(tiles, rows, nz)
        vmem = pl.BlockSpec(memory_space=pltpu.VMEM)
        hbm = pl.BlockSpec(memory_space=pltpu.HBM)
        any_spec = pl.BlockSpec(memory_space=pl.ANY)
        dma = pltpu.SemaphoreType.DMA
        f32 = jnp.float32
        fields, grad = pl.pallas_call(
            functools.partial(kernel, n, slabs, scale),
            out_shape=(
                pltpu.VMEM((2, 2, comps, xr + 2, nh, nz), f32),
                pltpu.VMEM(flat.shape, f32),
            ),
            in_specs=[any_spec] * 8,
            out_specs=(vmem, vmem),
            scratch_shapes=[
                pltpu.SMEM(wavelet.shape, f32),
                pltpu.SMEM(encoding.shape, jnp.int32),
                pltpu.SMEM(cells.shape, jnp.int32),
                pltpu.VMEM(depth.shape, jnp.int32),
                pltpu.VMEM(data.shape, f32),
                pltpu.VMEM((2, STEPS, 2, 3, nh, nz), f32),
                pltpu.VMEM((2, STEPS, 2, 3, nh, nz), f32),
                pltpu.VMEM((2, STEPS, 2, 3, nh, nz), f32),
                pltpu.VMEM((2, STEPS, 2, 3, nh, nz), f32),
                pltpu.VMEM((n, tiles, rows, nz), f32),
                pltpu.VMEM((nc, xr + 2, ny, nz), f32),
                pltpu.VMEM((2, nc, xr + 2, nh, nz), f32),
                pltpu.VMEM((xr, ny, nz), f32),
                pltpu.VMEM((STEPS, xr, ny, nz), f32),
                pltpu.VMEM((n, tiles, rows, nz), f32),
                pltpu.VMEM((L, tiles, rows, nz), f32),
                pltpu.VMEM((L, tiles, rows, nz), f32),
                pltpu.VMEM((L, tiles, rows, nz), f32),
                dma((12,)),
                dma((2, 3, 2 * STEPS)),
                dma((2, 3, 2 * STEPS)),
                dma((n,)),
                dma((n,)),
                dma((1,)),
                dma((L,)),
                dma((L,)),
                dma((L,)),
                dma((L,)),
                dma((L,)),
                dma((L,)),
                dma((L,)),
            ],
            compiler_params=pltpu.CompilerParams(
                collective_id=0, has_side_effects=True, vmem_limit_bytes=56 * 1024 * 1024
            ),
        )(wavelet, encoding, cells, depth, data, fwd, adj, flat)
        fwd_out, adj_out, grad = pl.pallas_call(
            write_out,
            out_shape=(
                pltpu.HBM(fwd.shape, f32),
                pltpu.HBM(adj.shape, f32),
                pltpu.HBM(flat.shape, f32),
            ),
            in_specs=[vmem, vmem],
            out_specs=(hbm, hbm, hbm),
            scratch_shapes=[dma((5,))],
            compiler_params=pltpu.CompilerParams(vmem_limit_bytes=8 * 1024 * 1024),
        )(fields, grad)
        return fwd_out, adj_out, grad.reshape(mats.shape)

    return jax.shard_map(
        body,
        mesh=mesh,
        in_specs=(
            P("shot", None, "slab", None, None),
            P("shot", None, "slab", None, None),
            P(None, "slab", "shot", None),
            P(),
            P("shot", None),
            P("shot", None),
            P("slab", None),
            P("shot", None, "slab", None),
        ),
        out_specs=(
            P("shot", None, "slab", None, None),
            P("shot", None, "slab", None, None),
            P(None, "slab", "shot", None),
        ),
        check_vma=False,
    )
```

```python
import functools

import jax
import jax.numpy as jnp
from jax import lax
from jax.experimental import pallas as pl
from jax.experimental.pallas import tpu as pltpu
from jax.sharding import PartitionSpec as P

STEPS = 4
STEP_SIZE = 0.25
PAD = 8
VX, VY, VZ, SXX, SYY, SZZ, SYZ, SXZ, SXY = range(9)
PAIRS = [(0, 0), (0, 1), (0, 2), (1, 1), (1, 2), (2, 2), (3, 3), (4, 4), (5, 5)]


def kernel(
    n,
    slabs,
    scale,
    wavelet_in,
    encoding_in,
    cells_in,
    depth_in,
    data_in,
    fwd_in,
    adj_in,
    mats_in,
    F,
    grad_out,
    wavelet,
    encoding,
    cells,
    depth,
    data,
    up_out,
    dn_out,
    up_got,
    dn_got,
    slots,
    mat,
    acc,
    image,
    inj,
    blocks,
    ry,
    rright,
    rleft,
    load_sem,
    halo_send,
    halo_recv,
    ag_recv,
    ag_send_z,
    ag_send_o,
    ag_send_y,
    rs_recv_y,
    rs_send_y,
    rs_recv_r,
    rs_send_r,
    rs_recv_l,
    rs_send_l,
):
    _, comps, xr, ny, nz = fwd_in.shape
    tiles, rows, _ = mats_in.shape
    nc = mat.shape[0]
    yb = ny // n
    group = rows // yb
    L = n // 2
    me = lax.axis_index("shot")
    slab = lax.axis_index("slab")
    lo = lax.rem(me, 2)
    hi = me // 2
    partner = hi * 2 + 1 - lo

    small = [
        pltpu.make_async_copy(src, dst, load_sem.at[3 + i])
        for i, (src, dst) in enumerate(
            [
                (wavelet_in, wavelet),
                (encoding_in, encoding),
                (cells_in, cells),
                (depth_in, depth),
                (data_in, data),
            ]
        )
    ]
    loads = [
        pltpu.make_async_copy(fwd_in.at[0], F.at[0, :, pl.ds(1, xr), pl.ds(PAD, ny)], load_sem.at[0]),
        pltpu.make_async_copy(adj_in.at[0], F.at[1, :, pl.ds(1, xr), pl.ds(PAD, ny)], load_sem.at[1]),
        pltpu.make_async_copy(mats_in, slots.at[me], load_sem.at[2]),
    ]
    for c in loads + small:
        c.start()

    def get(w, c, x, by=0):
        return F[w, c, x, pl.ds(PAD + by, ny)]

    def put(w, c, x, value):
        F[w, c, x, pl.ds(PAD, ny)] = value

    zero_layer = jnp.zeros((ny, nz), jnp.float32)
    mat[0, 0] = zero_layer
    mat[0, xr + 1] = zero_layer
    for w in range(2):
        put(w, VX, 0, zero_layer)
        put(w, VY, xr + 1, zero_layer)
        put(w, VZ, xr + 1, zero_layer)
        for x in range(1, xr + 1):
            for c in (SXY, SYZ, VY):
                F[w, c, x, pl.ds(0, PAD)] = jnp.zeros((PAD, nz), jnp.float32)
            for c in (SYY, VX, VZ):
                F[w, c, x, pl.ds(PAD + ny, PAD)] = jnp.zeros((PAD, nz), jnp.float32)
        for i in range(3):
            for t in range(STEPS):
                up_got[t, w, i] = zero_layer
                dn_got[t, w, i] = zero_layer

    def shot_id(index):
        return {"shot": index}

    def slab_id(index):
        return {"slab": index}

    MESH = pl.DeviceIdType.MESH
    barrier = pltpu.get_barrier_semaphore()

    def greet(cond, device):
        @pl.when(cond)
        def _():
            pl.semaphore_signal(barrier, inc=1, device_id=device, device_id_type=MESH)

    has_r = hi < L - 1
    has_l = hi > 0
    has_up = slab < slabs - 1
    has_dn = slab > 0
    pl.semaphore_signal(barrier, inc=1, device_id=shot_id(partner), device_id_type=MESH)
    greet(has_r, shot_id(me + 2))
    greet(has_l, shot_id(me - 2))
    greet(has_up, slab_id(slab + 1))
    greet(has_dn, slab_id(slab - 1))
    one = jnp.int32(1)
    nul = jnp.int32(0)
    count = (
        one
        + jnp.where(has_r, one, nul)
        + jnp.where(has_l, one, nul)
        + jnp.where(has_up, one, nul)
        + jnp.where(has_dn, one, nul)
    )
    pl.semaphore_wait(barrier, count)

    def remote(src, dst, ss, rs, device):
        return pltpu.make_async_remote_copy(
            src_ref=src,
            dst_ref=dst,
            send_sem=ss,
            recv_sem=rs,
            device_id=device,
            device_id_type=MESH,
        )

    def when(cond, fn):
        pl.when(cond)(fn)

    def to_partner(block, src):
        return remote(
            src, slots.at[block], ag_send_y.at[block // 2], ag_recv.at[block], shot_id(partner)
        )

    def to_line(block, src, by, sem):
        return remote(src, slots.at[block], sem, ag_recv.at[block], shot_id(me + 2 * by))

    own_r = to_line(me, mats_in, 1, ag_send_z.at[me])
    own_l = to_line(me, mats_in, -1, ag_send_o.at[0])
    own_p = to_partner(me, mats_in)
    when(has_r, own_r.start)
    when(has_l, own_l.start)
    own_p.start()

    inner = pl.ds(PAD, ny)

    def halo(kind, t):
        if kind == 0:
            up_src, up_dst = up_out.at[t], up_got.at[t]
            dn_src, dn_dst = dn_out.at[t], dn_got.at[t]
        elif kind == 1:
            up_src, up_dst = F.at[:, VX, xr, inner], F.at[:, VX, 0, inner]
            dn_src = F.at[:, pl.ds(VY, 2), 1, inner]
            dn_dst = F.at[:, pl.ds(VY, 2), xr + 1, inner]
        else:
            up_src, up_dst = mat.at[0, xr], mat.at[0, 0]
            dn_src, dn_dst = mat.at[0, 1], mat.at[0, xr + 1]
        up = remote(
            up_src, up_dst, halo_send.at[0, kind, t], halo_recv.at[0, kind, t], slab_id(slab + 1)
        )
        dn = remote(
            dn_src, dn_dst, halo_send.at[1, kind, t], halo_recv.at[1, kind, t], slab_id(slab - 1)
        )
        return up, dn

    def halo_start(kind, t):
        up, dn = halo(kind, t)
        when(has_up, up.start)
        when(has_dn, dn.start)

    def halo_wait(kind, t):
        up, dn = halo(kind, t)
        when(has_dn, up.wait_recv)
        when(has_up, dn.wait_recv)

    def halo_sent(kind, t):
        up, dn = halo(kind, t)
        when(has_up, up.wait_send)
        when(has_dn, dn.wait_send)

    for c in loads + small:
        c.wait()
    halo_start(1, 0)

    lane = lax.broadcasted_iota(jnp.int32, (ny, nz), 1)
    row = lax.broadcasted_iota(jnp.int32, (ny, nz), 0)

    def up_y(w, c, x):
        return get(w, c, x, 1) - get(w, c, x)

    def down_y(w, c, x):
        return get(w, c, x) - get(w, c, x, -1)

    def up_z(a):
        return jnp.where(lane == nz - 1, 0.0, pltpu.roll(a, nz - 1, 1)) - a

    def down_z(a):
        return a - jnp.where(lane == 0, 0.0, pltpu.roll(a, 1, 1))

    def pack(t):
        for w in range(2):
            sxz = get(w, SXZ, xr)
            up_out[t, w, 0] = down_y(w, SXY, xr) + down_z(sxz) - get(w, SXX, xr)
            up_out[t, w, 1] = sxz
            up_out[t, w, 2] = get(w, SXY, xr)
            dn_out[t, w, 0] = get(w, SXY, 1) + up_y(w, SYY, 1) + down_z(get(w, SYZ, 1))
            dn_out[t, w, 1] = get(w, SXZ, 1) + down_y(w, SYZ, 1) + up_z(get(w, SZZ, 1))
            dn_out[t, w, 2] = get(w, SXX, 1)
        halo_start(0, t)

    def unpack(t):
        halo_wait(0, t)
        for w in range(2):
            put(w, SXZ, 0, up_got[t, w, 1])
            put(w, SXY, 0, up_got[t, w, 2])
            put(w, SXX, xr + 1, dn_got[t, w, 2])

    def ghosts(t):
        top = xr + 1
        for w in range(2):
            fx = get(w, SXX, 1) + up_got[t, w, 0]
            fy = dn_got[t, w, 0] - get(w, SXY, xr)
            fz = dn_got[t, w, 1] - get(w, SXZ, xr)
            put(w, VX, 0, get(w, VX, 0) + mat[0, 0] * fx)
            put(w, VY, top, get(w, VY, top) + mat[0, top] * fy)
            put(w, VZ, top, get(w, VZ, top) + mat[0, top] * fz)

    pack(0)

    eye = lax.broadcasted_iota(jnp.int32, (ny, ny), 0) == lax.broadcasted_iota(
        jnp.int32, (ny, ny), 1
    )

    def column(r):
        wide = jnp.broadcast_to(r, (ny, ny))
        return jnp.sum(jnp.where(eye, wide, 0.0), axis=1, keepdims=True)

    def prepare(x, carry):
        cell = ((slab * xr + x) * ny + row) * nz + lane
        total = jnp.zeros((ny, nz), jnp.float32)
        for j in range(cells.shape[1]):
            sign = (2 * encoding[0, j] - 1).astype(jnp.float32)
            total = total + jnp.where(cell == cells[0, j], sign, 0.0)
        image[x] = total
        hit = lane.astype(jnp.float32) == column(depth[pl.ds(x, 1), :].astype(jnp.float32))
        for t in range(STEPS):
            inj[t, x] = jnp.where(hit, column(data[0, t, pl.ds(x, 1), :]), 0.0)
        return carry

    lax.fori_loop(0, xr, prepare, 0)

    for k in range(1, L):
        def right_moving(k=k):
            b = me - 2 * k
            ref = slots.at[b]
            to_line(b, ref, 1, ag_send_z.at[b]).wait_recv()
            when(has_r, to_line(b, ref, 1, ag_send_z.at[b]).start)
            to_partner(b, ref).start()

        def left_moving(k=k):
            b = me + 2 * k
            ref = slots.at[b]
            to_line(b, ref, -1, ag_send_z.at[b]).wait_recv()
            when(has_l, to_line(b, ref, -1, ag_send_z.at[b]).start)
            to_partner(b, ref).start()

        when(hi >= k, right_moving)
        when(hi + k < L, left_moving)
    for h in range(L):
        b = h * 2 + 1 - lo
        to_partner(b, slots.at[b]).wait_recv()

    def assemble(xg, carry):
        for c in range(nc):
            held = [slots[i, c * (xr // group) + xg] for i in range(n)]
            for j in range(group):
                whole = jnp.concatenate([h[j * yb : (j + 1) * yb] for h in held], axis=0)
                mat[c, xg * group + j + 1] = whole * STEP_SIZE
        return carry

    lax.fori_loop(0, xr // group, assemble, 0)
    halo_start(2, 0)

    def velocity_layer(t, x):
        forces = []
        old = []
        for w in range(2):
            sxx, sxy, sxz = get(w, SXX, x), get(w, SXY, x), get(w, SXZ, x)
            syz = get(w, SYZ, x)
            fx = (get(w, SXX, x + 1) - sxx) + down_y(w, SXY, x) + down_z(sxz)
            fy = (sxy - get(w, SXY, x - 1)) + up_y(w, SYY, x) + down_z(syz)
            fz = (sxz - get(w, SXZ, x - 1)) + down_y(w, SYZ, x) + up_z(get(w, SZZ, x))
            forces.append([fx, fy, fz])
            old.append([get(w, VX, x), get(w, VY, x), get(w, VZ, x)])
        term = (
            forces[0][0] * old[1][0] + forces[0][1] * old[1][1] + forces[0][2] * old[1][2]
        )
        acc[0, x] = term if t == 0 else acc[0, x] + term
        buoy = mat[0, x]
        for w in range(2):
            for c in range(3):
                put(w, c, x, old[w][c] + buoy * forces[w][c])

    def strain_of(w, x):
        vx, vy, vz = get(w, VX, x), get(w, VY, x), get(w, VZ, x)
        return [
            vx - get(w, VX, x - 1),
            down_y(w, VY, x),
            down_z(vz),
            up_z(vy) + up_y(w, VZ, x),
            up_z(vx) + (get(w, VZ, x + 1) - vz),
            up_y(w, VX, x) + (get(w, VY, x + 1) - vy),
        ]

    def add_terms(t, x, f, a):
        for i, (p, q) in enumerate(PAIRS):
            term = f[p] * a[q]
            if p != q:
                term = term + f[q] * a[p]
            if t > 0:
                term = term + acc[i + 1, x]
            acc[i + 1, x] = term

    def put_blocks(xg):
        for c in range(nc):
            held = [acc[c, xg * group + j + 1] * scale for j in range(group)]
            for i in range(n):
                blocks[i, c * (xr // group) + xg] = jnp.concatenate(
                    [h[i * yb : (i + 1) * yb] for h in held], axis=0
                )

    def stress_layer(t, x, strains):
        m = [mat[c, x] for c in range(nc)]
        for w in range(2):
            exx, eyy, ezz, gyz, gxz, gxy = strains[w]
            extra = wavelet[t] * image[x - 1] if w == 0 else inj[t, x - 1]
            for c, change in (
                (SXX, m[1] * exx + m[2] * eyy + m[3] * ezz),
                (SYY, m[2] * exx + m[4] * eyy + m[5] * ezz),
                (SZZ, m[3] * exx + m[5] * eyy + m[6] * ezz + extra),
                (SYZ, m[7] * gyz),
                (SXZ, m[8] * gxz),
                (SXY, m[9] * gxy),
            ):
                put(w, c, x, get(w, c, x) + change)

    def over(start, stop, step, fn):
        def one_layer(j, carry):
            fn(start + j * step)
            return carry

        lax.fori_loop(0, (stop - start + step - 1) // step, one_layer, 0, unroll=2)

    def interior(fn):
        over(2, xr, 1, fn)

    def rims(fn):
        over(1, xr + 1, xr - 1, fn)

    for t in range(STEPS):
        last = t == STEPS - 1
        interior(functools.partial(velocity_layer, t))
        unpack(t)
        if t == 0:
            halo_sent(1, 0)
        rims(functools.partial(velocity_layer, t))
        if t == 0:
            halo_wait(1, 0)
            halo_wait(2, 0)
        ghosts(t)

        def both(x, t=t, last=last):
            strains = [strain_of(w, x) for w in range(2)]
            add_terms(t, x, strains[0], strains[1])
            if not last:
                stress_layer(t, x, strains)

        rims(both)
        if not last:
            pack(t + 1)
        interior(both)
    over(0, xr // group, 1, put_blocks)

    def rs_y(d):
        return remote(
            blocks.at[d * 2 + 1 - lo],
            ry.at[d],
            rs_send_y.at[d],
            rs_recv_y.at[d],
            shot_id(partner),
        )

    def rs_r(d):
        return remote(
            ry.at[d], rright.at[d], rs_send_r.at[d], rs_recv_r.at[d], shot_id(me + 2)
        )

    def rs_l(d):
        return remote(ry.at[d], rleft.at[d], rs_send_l.at[d], rs_recv_l.at[d], shot_id(me - 2))

    for k in range(L - 1, 0, -1):
        when(hi + k < L, lambda k=k: rs_y(hi + k).start())
        when(hi >= k, lambda k=k: rs_y(hi - k).start())
    rs_y(hi).start()

    over(1, xr + 1, 1, lambda x: stress_layer(STEPS - 1, x, [strain_of(w, x) for w in range(2)]))

    def add_into(d, extra, target):
        def one_layer(x, carry):
            for c in range(nc):
                i = x * nc + c
                total = ry[d, i] + blocks[d * 2 + lo, i]
                if extra is not None:
                    total = total + extra[d, i]
                target[i] = total
            return carry

        lax.fori_loop(0, tiles // nc, one_layer, 0)

    for k in range(L - 1, 0, -1):
        def send_right(k=k):
            d = hi + k
            rs_y(d).wait_recv()

            def plus():
                rs_r(d).wait_recv()
                add_into(d, rright, ry.at[d])

            when(has_l, plus)
            when(hi == 0, lambda: add_into(d, None, ry.at[d]))
            rs_r(d).start()

        def send_left(k=k):
            d = hi - k
            rs_y(d).wait_recv()

            def plus():
                rs_l(d).wait_recv()
                add_into(d, rleft, ry.at[d])

            when(has_r, plus)
            when(hi == L - 1, lambda: add_into(d, None, ry.at[d]))
            rs_l(d).start()

        when(hi + k < L, send_right)
        when(hi >= k, send_left)

    rs_y(hi).wait_recv()
    add_into(hi, None, grad_out)

    def take(ref):
        def one_layer(x, carry):
            for c in range(nc):
                i = x * nc + c
                grad_out[i] = grad_out[i] + ref[hi, i]
            return carry

        lax.fori_loop(0, tiles // nc, one_layer, 0)

    def from_left():
        rs_r(hi).wait_recv()
        take(rright)

    def from_right():
        rs_l(hi).wait_recv()
        take(rleft)

    when(has_l, from_left)
    when(has_r, from_right)

    when(has_r, own_r.wait_send)
    when(has_l, own_l.wait_send)
    own_p.wait_send()
    for k in range(1, L):
        def right_sent(k=k):
            b = me - 2 * k
            when(has_r, to_line(b, slots.at[b], 1, ag_send_z.at[b]).wait_send)
            to_partner(b, slots.at[b]).wait_send()

        def left_sent(k=k):
            b = me + 2 * k
            when(has_l, to_line(b, slots.at[b], -1, ag_send_z.at[b]).wait_send)
            to_partner(b, slots.at[b]).wait_send()

        when(hi >= k, right_sent)
        when(hi + k < L, left_sent)
        when(hi + k < L, lambda k=k: rs_y(hi + k).wait_send())
        when(hi >= k, lambda k=k: rs_y(hi - k).wait_send())
        when(hi + k < L, lambda k=k: rs_r(hi + k).wait_send())
        when(hi >= k, lambda k=k: rs_l(hi - k).wait_send())
    rs_y(hi).wait_send()
    for t in range(STEPS):
        halo_sent(0, t)
    halo_sent(2, 0)


def write_out(F, grad, fwd_out, adj_out, grad_out, sem):
    xr, ny = fwd_out.shape[2:4]
    comps = fwd_out.shape[1]
    half = comps // 2
    copies = [pltpu.make_async_copy(grad, grad_out, sem.at[4])]
    for w, out in ((0, fwd_out), (1, adj_out)):
        for j, (first, count) in enumerate(((0, half), (half, comps - half))):
            copies.append(
                pltpu.make_async_copy(
                    F.at[w, pl.ds(first, count), pl.ds(1, xr), pl.ds(PAD, ny)],
                    out.at[0, pl.ds(first, count)],
                    sem.at[2 * w + j],
                )
            )
    for c in copies:
        c.start()
    for c in copies:
        c.wait()


def solution(mesh):
    n = mesh.shape["shot"]
    slabs = mesh.shape["slab"]

    def body(fwd, adj, mats, wavelet, encoding, cells, depth, data):
        shots, comps, xr, ny, nz = fwd.shape
        nc, _, yb, _ = mats.shape
        L = n // 2
        scale = float(shots * n * STEPS) ** (-0.5)
        rows = max(8, yb)
        tiles = nc * xr * yb // rows
        flat = mats.reshape(tiles, rows, nz)
        vmem = pl.BlockSpec(memory_space=pltpu.VMEM)
        hbm = pl.BlockSpec(memory_space=pltpu.HBM)
        any_spec = pl.BlockSpec(memory_space=pl.ANY)
        dma = pltpu.SemaphoreType.DMA
        f32 = jnp.float32
        fields, grad = pl.pallas_call(
            functools.partial(kernel, n, slabs, scale),
            out_shape=(
                pltpu.VMEM((2, comps, xr + 2, ny + 2 * PAD, nz), f32),
                pltpu.VMEM(flat.shape, f32),
            ),
            in_specs=[any_spec] * 8,
            out_specs=(vmem, vmem),
            scratch_shapes=[
                pltpu.SMEM(wavelet.shape, f32),
                pltpu.SMEM(encoding.shape, jnp.int32),
                pltpu.SMEM(cells.shape, jnp.int32),
                pltpu.VMEM(depth.shape, jnp.int32),
                pltpu.VMEM(data.shape, f32),
                pltpu.VMEM((STEPS, 2, 3, ny, nz), f32),
                pltpu.VMEM((STEPS, 2, 3, ny, nz), f32),
                pltpu.VMEM((STEPS, 2, 3, ny, nz), f32),
                pltpu.VMEM((STEPS, 2, 3, ny, nz), f32),
                pltpu.VMEM((n, tiles, rows, nz), f32),
                pltpu.VMEM((nc, xr + 2, ny, nz), f32),
                pltpu.VMEM((nc, xr + 2, ny, nz), f32),
                pltpu.VMEM((xr, ny, nz), f32),
                pltpu.VMEM((STEPS, xr, ny, nz), f32),
                pltpu.VMEM((n, tiles, rows, nz), f32),
                pltpu.VMEM((L, tiles, rows, nz), f32),
                pltpu.VMEM((L, tiles, rows, nz), f32),
                pltpu.VMEM((L, tiles, rows, nz), f32),
                dma((8,)),
                dma((2, 3, STEPS)),
                dma((2, 3, STEPS)),
                dma((n,)),
                dma((n,)),
                dma((1,)),
                dma((L,)),
                dma((L,)),
                dma((L,)),
                dma((L,)),
                dma((L,)),
                dma((L,)),
                dma((L,)),
            ],
            compiler_params=pltpu.CompilerParams(
                collective_id=0, has_side_effects=True, vmem_limit_bytes=56 * 1024 * 1024
            ),
        )(wavelet, encoding, cells, depth, data, fwd, adj, flat)
        fwd_out, adj_out, grad = pl.pallas_call(
            write_out,
            out_shape=(
                pltpu.HBM(fwd.shape, f32),
                pltpu.HBM(adj.shape, f32),
                pltpu.HBM(flat.shape, f32),
            ),
            in_specs=[vmem, vmem],
            out_specs=(hbm, hbm, hbm),
            scratch_shapes=[dma((5,))],
            compiler_params=pltpu.CompilerParams(vmem_limit_bytes=8 * 1024 * 1024),
        )(fields, grad)
        return fwd_out, adj_out, grad.reshape(mats.shape)

    return jax.shard_map(
        body,
        mesh=mesh,
        in_specs=(
            P("shot", None, "slab", None, None),
            P("shot", None, "slab", None, None),
            P(None, "slab", "shot", None),
            P(),
            P("shot", None),
            P("shot", None),
            P("slab", None),
            P("shot", None, "slab", None),
        ),
        out_specs=(
            P("shot", None, "slab", None, None),
            P("shot", None, "slab", None, None),
            P(None, "slab", "shot", None),
        ),
        check_vma=False,
    )
```

```python
import functools

import jax
import jax.numpy as jnp
from jax import lax
from jax.experimental import pallas as pl
from jax.experimental.pallas import tpu as pltpu
from jax.sharding import PartitionSpec as P

STEPS = 4
STEP_SIZE = 0.25
PAD = 8
VX, VY, VZ, SXX, SYY, SZZ, SYZ, SXZ, SXY = range(9)
PAIRS = [(0, 0), (0, 1), (0, 2), (1, 1), (1, 2), (2, 2), (3, 3), (4, 4), (5, 5)]


def kernel(
    n,
    slabs,
    scale,
    wavelet_in,
    encoding_in,
    cells_in,
    depth_in,
    data_in,
    fwd_in,
    adj_in,
    mats_in,
    F,
    grad_out,
    wavelet,
    encoding,
    cells,
    depth,
    data,
    up_out,
    dn_out,
    up_got,
    dn_got,
    slots,
    mat,
    acc,
    image,
    inj,
    blocks,
    ry,
    rright,
    rleft,
    load_sem,
    halo_send,
    halo_recv,
    ag_recv,
    ag_send_z,
    ag_send_o,
    ag_send_y,
    rs_recv_y,
    rs_send_y,
    rs_recv_r,
    rs_send_r,
    rs_recv_l,
    rs_send_l,
):
    _, comps, xr, ny, nz = fwd_in.shape
    tiles, rows, _ = mats_in.shape
    nc = mat.shape[0]
    yb = ny // n
    group = rows // yb
    L = n // 2
    me = lax.axis_index("shot")
    slab = lax.axis_index("slab")
    lo = lax.rem(me, 2)
    hi = me // 2
    partner = hi * 2 + 1 - lo

    small = [
        pltpu.make_async_copy(src, dst, load_sem.at[3 + i])
        for i, (src, dst) in enumerate(
            [
                (wavelet_in, wavelet),
                (encoding_in, encoding),
                (cells_in, cells),
                (depth_in, depth),
                (data_in, data),
            ]
        )
    ]
    loads = [
        pltpu.make_async_copy(fwd_in.at[0], F.at[0, :, pl.ds(1, xr), pl.ds(PAD, ny)], load_sem.at[0]),
        pltpu.make_async_copy(adj_in.at[0], F.at[1, :, pl.ds(1, xr), pl.ds(PAD, ny)], load_sem.at[1]),
        pltpu.make_async_copy(mats_in, slots.at[me], load_sem.at[2]),
    ]
    for c in loads + small:
        c.start()

    def get(w, c, x, by=0):
        return F[w, c, x, pl.ds(PAD + by, ny)]

    def put(w, c, x, value):
        F[w, c, x, pl.ds(PAD, ny)] = value

    zero_layer = jnp.zeros((ny, nz), jnp.float32)
    mat[0, 0] = zero_layer
    mat[0, xr + 1] = zero_layer
    for w in range(2):
        put(w, VX, 0, zero_layer)
        put(w, VY, xr + 1, zero_layer)
        put(w, VZ, xr + 1, zero_layer)
        for x in range(1, xr + 1):
            for c in (SXY, SYZ, VY):
                F[w, c, x, pl.ds(0, PAD)] = jnp.zeros((PAD, nz), jnp.float32)
            for c in (SYY, VX, VZ):
                F[w, c, x, pl.ds(PAD + ny, PAD)] = jnp.zeros((PAD, nz), jnp.float32)
        for i in range(3):
            for t in range(STEPS):
                up_got[t, w, i] = zero_layer
                dn_got[t, w, i] = zero_layer

    def shot_id(index):
        return {"shot": index}

    def slab_id(index):
        return {"slab": index}

    MESH = pl.DeviceIdType.MESH
    barrier = pltpu.get_barrier_semaphore()

    def greet(cond, device):
        @pl.when(cond)
        def _():
            pl.semaphore_signal(barrier, inc=1, device_id=device, device_id_type=MESH)

    has_r = hi < L - 1
    has_l = hi > 0
    has_up = slab < slabs - 1
    has_dn = slab > 0
    pl.semaphore_signal(barrier, inc=1, device_id=shot_id(partner), device_id_type=MESH)
    greet(has_r, shot_id(me + 2))
    greet(has_l, shot_id(me - 2))
    greet(has_up, slab_id(slab + 1))
    greet(has_dn, slab_id(slab - 1))
    one = jnp.int32(1)
    nul = jnp.int32(0)
    count = (
        one
        + jnp.where(has_r, one, nul)
        + jnp.where(has_l, one, nul)
        + jnp.where(has_up, one, nul)
        + jnp.where(has_dn, one, nul)
    )
    pl.semaphore_wait(barrier, count)

    def remote(src, dst, ss, rs, device):
        return pltpu.make_async_remote_copy(
            src_ref=src,
            dst_ref=dst,
            send_sem=ss,
            recv_sem=rs,
            device_id=device,
            device_id_type=MESH,
        )

    def when(cond, fn):
        pl.when(cond)(fn)

    def to_partner(block, src):
        return remote(
            src, slots.at[block], ag_send_y.at[block // 2], ag_recv.at[block], shot_id(partner)
        )

    def to_line(block, src, by, sem):
        return remote(src, slots.at[block], sem, ag_recv.at[block], shot_id(me + 2 * by))

    own_r = to_line(me, mats_in, 1, ag_send_z.at[me])
    own_l = to_line(me, mats_in, -1, ag_send_o.at[0])
    own_p = to_partner(me, mats_in)
    when(has_r, own_r.start)
    when(has_l, own_l.start)
    own_p.start()

    inner = pl.ds(PAD, ny)

    def halo(kind, t):
        if kind == 0:
            up_src, up_dst = up_out.at[t], up_got.at[t]
            dn_src, dn_dst = dn_out.at[t], dn_got.at[t]
        elif kind == 1:
            up_src, up_dst = F.at[:, VX, xr, inner], F.at[:, VX, 0, inner]
            dn_src = F.at[:, pl.ds(VY, 2), 1, inner]
            dn_dst = F.at[:, pl.ds(VY, 2), xr + 1, inner]
        else:
            up_src, up_dst = mat.at[0, xr], mat.at[0, 0]
            dn_src, dn_dst = mat.at[0, 1], mat.at[0, xr + 1]
        up = remote(
            up_src, up_dst, halo_send.at[0, kind, t], halo_recv.at[0, kind, t], slab_id(slab + 1)
        )
        dn = remote(
            dn_src, dn_dst, halo_send.at[1, kind, t], halo_recv.at[1, kind, t], slab_id(slab - 1)
        )
        return up, dn

    def halo_start(kind, t):
        up, dn = halo(kind, t)
        when(has_up, up.start)
        when(has_dn, dn.start)

    def halo_wait(kind, t):
        up, dn = halo(kind, t)
        when(has_dn, up.wait_recv)
        when(has_up, dn.wait_recv)

    def halo_sent(kind, t):
        up, dn = halo(kind, t)
        when(has_up, up.wait_send)
        when(has_dn, dn.wait_send)

    for c in loads + small:
        c.wait()
    halo_start(1, 0)

    lane = lax.broadcasted_iota(jnp.int32, (ny, nz), 1)
    row = lax.broadcasted_iota(jnp.int32, (ny, nz), 0)

    def up_y(w, c, x):
        return get(w, c, x, 1) - get(w, c, x)

    def down_y(w, c, x):
        return get(w, c, x) - get(w, c, x, -1)

    def up_z(a):
        return jnp.where(lane == nz - 1, 0.0, pltpu.roll(a, nz - 1, 1)) - a

    def down_z(a):
        return a - jnp.where(lane == 0, 0.0, pltpu.roll(a, 1, 1))

    def pack(t):
        for w in range(2):
            sxz = get(w, SXZ, xr)
            up_out[t, w, 0] = down_y(w, SXY, xr) + down_z(sxz) - get(w, SXX, xr)
            up_out[t, w, 1] = sxz
            up_out[t, w, 2] = get(w, SXY, xr)
            dn_out[t, w, 0] = get(w, SXY, 1) + up_y(w, SYY, 1) + down_z(get(w, SYZ, 1))
            dn_out[t, w, 1] = get(w, SXZ, 1) + down_y(w, SYZ, 1) + up_z(get(w, SZZ, 1))
            dn_out[t, w, 2] = get(w, SXX, 1)
        halo_start(0, t)

    def unpack(t):
        halo_wait(0, t)
        for w in range(2):
            put(w, SXZ, 0, up_got[t, w, 1])
            put(w, SXY, 0, up_got[t, w, 2])
            put(w, SXX, xr + 1, dn_got[t, w, 2])

    def ghosts(t):
        top = xr + 1
        for w in range(2):
            fx = get(w, SXX, 1) + up_got[t, w, 0]
            fy = dn_got[t, w, 0] - get(w, SXY, xr)
            fz = dn_got[t, w, 1] - get(w, SXZ, xr)
            put(w, VX, 0, get(w, VX, 0) + mat[0, 0] * fx)
            put(w, VY, top, get(w, VY, top) + mat[0, top] * fy)
            put(w, VZ, top, get(w, VZ, top) + mat[0, top] * fz)

    pack(0)

    eye = lax.broadcasted_iota(jnp.int32, (ny, ny), 0) == lax.broadcasted_iota(
        jnp.int32, (ny, ny), 1
    )

    def column(r):
        wide = jnp.broadcast_to(r, (ny, ny))
        return jnp.sum(jnp.where(eye, wide, 0.0), axis=1, keepdims=True)

    def prepare(x, carry):
        cell = ((slab * xr + x) * ny + row) * nz + lane
        total = jnp.zeros((ny, nz), jnp.float32)
        for j in range(cells.shape[1]):
            sign = (2 * encoding[0, j] - 1).astype(jnp.float32)
            total = total + jnp.where(cell == cells[0, j], sign, 0.0)
        image[x] = total
        hit = lane.astype(jnp.float32) == column(depth[pl.ds(x, 1), :].astype(jnp.float32))
        for t in range(STEPS):
            inj[t, x] = jnp.where(hit, column(data[0, t, pl.ds(x, 1), :]), 0.0)
        return carry

    lax.fori_loop(0, xr, prepare, 0)

    for k in range(1, L):
        def right_moving(k=k):
            b = me - 2 * k
            ref = slots.at[b]
            to_line(b, ref, 1, ag_send_z.at[b]).wait_recv()
            when(has_r, to_line(b, ref, 1, ag_send_z.at[b]).start)
            to_partner(b, ref).start()

        def left_moving(k=k):
            b = me + 2 * k
            ref = slots.at[b]
            to_line(b, ref, -1, ag_send_z.at[b]).wait_recv()
            when(has_l, to_line(b, ref, -1, ag_send_z.at[b]).start)
            to_partner(b, ref).start()

        when(hi >= k, right_moving)
        when(hi + k < L, left_moving)
    for h in range(L):
        b = h * 2 + 1 - lo
        to_partner(b, slots.at[b]).wait_recv()

    def assemble(xg, carry):
        for c in range(nc):
            held = [slots[i, c * (xr // group) + xg] for i in range(n)]
            for j in range(group):
                whole = jnp.concatenate([h[j * yb : (j + 1) * yb] for h in held], axis=0)
                mat[c, xg * group + j + 1] = whole * STEP_SIZE
        return carry

    lax.fori_loop(0, xr // group, assemble, 0)
    halo_start(2, 0)

    def velocity_layer(t, x):
        forces = []
        old = []
        for w in range(2):
            sxx, sxy, sxz = get(w, SXX, x), get(w, SXY, x), get(w, SXZ, x)
            syz = get(w, SYZ, x)
            fx = (get(w, SXX, x + 1) - sxx) + down_y(w, SXY, x) + down_z(sxz)
            fy = (sxy - get(w, SXY, x - 1)) + up_y(w, SYY, x) + down_z(syz)
            fz = (sxz - get(w, SXZ, x - 1)) + down_y(w, SYZ, x) + up_z(get(w, SZZ, x))
            forces.append([fx, fy, fz])
            old.append([get(w, VX, x), get(w, VY, x), get(w, VZ, x)])
        term = (
            forces[0][0] * old[1][0] + forces[0][1] * old[1][1] + forces[0][2] * old[1][2]
        )
        acc[0, x] = term if t == 0 else acc[0, x] + term
        buoy = mat[0, x]
        for w in range(2):
            for c in range(3):
                put(w, c, x, old[w][c] + buoy * forces[w][c])

    def strain_of(w, x):
        vx, vy, vz = get(w, VX, x), get(w, VY, x), get(w, VZ, x)
        return [
            vx - get(w, VX, x - 1),
            down_y(w, VY, x),
            down_z(vz),
            up_z(vy) + up_y(w, VZ, x),
            up_z(vx) + (get(w, VZ, x + 1) - vz),
            up_y(w, VX, x) + (get(w, VY, x + 1) - vy),
        ]

    def add_terms(t, x, f, a):
        for i, (p, q) in enumerate(PAIRS):
            term = f[p] * a[q]
            if p != q:
                term = term + f[q] * a[p]
            if t > 0:
                term = term + acc[i + 1, x]
            acc[i + 1, x] = term

    def put_blocks(xg):
        for c in range(nc):
            held = [acc[c, xg * group + j + 1] * scale for j in range(group)]
            for i in range(n):
                blocks[i, c * (xr // group) + xg] = jnp.concatenate(
                    [h[i * yb : (i + 1) * yb] for h in held], axis=0
                )

    def stress_layer(t, x, strains):
        m = [mat[c, x] for c in range(nc)]
        for w in range(2):
            exx, eyy, ezz, gyz, gxz, gxy = strains[w]
            extra = wavelet[t] * image[x - 1] if w == 0 else inj[t, x - 1]
            for c, change in (
                (SXX, m[1] * exx + m[2] * eyy + m[3] * ezz),
                (SYY, m[2] * exx + m[4] * eyy + m[5] * ezz),
                (SZZ, m[3] * exx + m[5] * eyy + m[6] * ezz + extra),
                (SYZ, m[7] * gyz),
                (SXZ, m[8] * gxz),
                (SXY, m[9] * gxy),
            ):
                put(w, c, x, get(w, c, x) + change)

    def over(start, stop, step, fn):
        def one_layer(j, carry):
            fn(start + j * step)
            return carry

        lax.fori_loop(0, (stop - start + step - 1) // step, one_layer, 0, unroll=2)

    def interior(fn):
        over(2, xr, 1, fn)

    def rims(fn):
        over(1, xr + 1, xr - 1, fn)

    for t in range(STEPS):
        last = t == STEPS - 1
        interior(functools.partial(velocity_layer, t))
        unpack(t)
        if t == 0:
            halo_sent(1, 0)
        rims(functools.partial(velocity_layer, t))
        if t == 0:
            halo_wait(1, 0)
            halo_wait(2, 0)
        ghosts(t)

        def both(x, t=t, last=last):
            strains = [strain_of(w, x) for w in range(2)]
            add_terms(t, x, strains[0], strains[1])
            if not last:
                stress_layer(t, x, strains)

        rims(both)
        if not last:
            pack(t + 1)
        interior(both)
    over(0, xr // group, 1, put_blocks)

    def rs_y(d):
        return remote(
            blocks.at[d * 2 + 1 - lo],
            ry.at[d],
            rs_send_y.at[d],
            rs_recv_y.at[d],
            shot_id(partner),
        )

    def rs_r(d):
        return remote(
            ry.at[d], rright.at[d], rs_send_r.at[d], rs_recv_r.at[d], shot_id(me + 2)
        )

    def rs_l(d):
        return remote(ry.at[d], rleft.at[d], rs_send_l.at[d], rs_recv_l.at[d], shot_id(me - 2))

    events = []
    seen = nul
    for k in range(L - 1, -1, -1):
        for sign in (1, -1) if k > 0 else (1,):
            d = hi + sign * k
            valid = (d >= 0) & (d < L)
            events.append((k, sign, d, valid, seen))
            seen = seen + jnp.where(valid, one, nul)

    def start_y(wanted, also):
        for _, _, d, valid, seen in events:
            when(also & valid & (seen == wanted), lambda d=d: rs_y(d).start())

    start_y(nul, hi >= 0)
    start_y(one, hi >= 0)

    over(1, xr + 1, 1, lambda x: stress_layer(STEPS - 1, x, [strain_of(w, x) for w in range(2)]))

    def add_into(d, extra, target):
        def one_layer(x, carry):
            for c in range(nc):
                i = x * nc + c
                total = ry[d, i] + blocks[d * 2 + lo, i]
                if extra is not None:
                    total = total + extra[d, i]
                target[i] = total
            return carry

        lax.fori_loop(0, tiles // nc, one_layer, 0)

    def send_line(d, sign):
        copy, held, more = (rs_r, rright, has_l) if sign > 0 else (rs_l, rleft, has_r)
        rs_y(d).wait_recv()

        def plus():
            copy(d).wait_recv()
            add_into(d, held, ry.at[d])

        when(more, plus)
        when(jnp.logical_not(more), lambda: add_into(d, None, ry.at[d]))
        copy(d).start()

    for k, sign, d, valid, seen in events:
        if k > 0:
            when(valid, functools.partial(send_line, d, sign))
            start_y(seen + 2, valid)

    rs_y(hi).wait_recv()
    add_into(hi, None, grad_out)

    def take(ref):
        def one_layer(x, carry):
            for c in range(nc):
                i = x * nc + c
                grad_out[i] = grad_out[i] + ref[hi, i]
            return carry

        lax.fori_loop(0, tiles // nc, one_layer, 0)

    def from_left():
        rs_r(hi).wait_recv()
        take(rright)

    def from_right():
        rs_l(hi).wait_recv()
        take(rleft)

    when(has_l, from_left)
    when(has_r, from_right)

    when(has_r, own_r.wait_send)
    when(has_l, own_l.wait_send)
    own_p.wait_send()
    for k in range(1, L):
        def right_sent(k=k):
            b = me - 2 * k
            when(has_r, to_line(b, slots.at[b], 1, ag_send_z.at[b]).wait_send)
            to_partner(b, slots.at[b]).wait_send()

        def left_sent(k=k):
            b = me + 2 * k
            when(has_l, to_line(b, slots.at[b], -1, ag_send_z.at[b]).wait_send)
            to_partner(b, slots.at[b]).wait_send()

        when(hi >= k, right_sent)
        when(hi + k < L, left_sent)
        when(hi + k < L, lambda k=k: rs_y(hi + k).wait_send())
        when(hi >= k, lambda k=k: rs_y(hi - k).wait_send())
        when(hi + k < L, lambda k=k: rs_r(hi + k).wait_send())
        when(hi >= k, lambda k=k: rs_l(hi - k).wait_send())
    rs_y(hi).wait_send()
    for t in range(STEPS):
        halo_sent(0, t)
    halo_sent(2, 0)


def write_out(F, grad, fwd_out, adj_out, grad_out, sem):
    xr, ny = fwd_out.shape[2:4]
    comps = fwd_out.shape[1]
    half = comps // 2
    copies = [pltpu.make_async_copy(grad, grad_out, sem.at[4])]
    for w, out in ((0, fwd_out), (1, adj_out)):
        for j, (first, count) in enumerate(((0, half), (half, comps - half))):
            copies.append(
                pltpu.make_async_copy(
                    F.at[w, pl.ds(first, count), pl.ds(1, xr), pl.ds(PAD, ny)],
                    out.at[0, pl.ds(first, count)],
                    sem.at[2 * w + j],
                )
            )
    for c in copies:
        c.start()
    for c in copies:
        c.wait()


def solution(mesh):
    n = mesh.shape["shot"]
    slabs = mesh.shape["slab"]

    def body(fwd, adj, mats, wavelet, encoding, cells, depth, data):
        shots, comps, xr, ny, nz = fwd.shape
        nc, _, yb, _ = mats.shape
        L = n // 2
        scale = float(shots * n * STEPS) ** (-0.5)
        rows = max(8, yb)
        tiles = nc * xr * yb // rows
        flat = mats.reshape(tiles, rows, nz)
        vmem = pl.BlockSpec(memory_space=pltpu.VMEM)
        hbm = pl.BlockSpec(memory_space=pltpu.HBM)
        any_spec = pl.BlockSpec(memory_space=pl.ANY)
        dma = pltpu.SemaphoreType.DMA
        f32 = jnp.float32
        fields, grad = pl.pallas_call(
            functools.partial(kernel, n, slabs, scale),
            out_shape=(
                pltpu.VMEM((2, comps, xr + 2, ny + 2 * PAD, nz), f32),
                pltpu.VMEM(flat.shape, f32),
            ),
            in_specs=[any_spec] * 8,
            out_specs=(vmem, vmem),
            scratch_shapes=[
                pltpu.SMEM(wavelet.shape, f32),
                pltpu.SMEM(encoding.shape, jnp.int32),
                pltpu.SMEM(cells.shape, jnp.int32),
                pltpu.VMEM(depth.shape, jnp.int32),
                pltpu.VMEM(data.shape, f32),
                pltpu.VMEM((STEPS, 2, 3, ny, nz), f32),
                pltpu.VMEM((STEPS, 2, 3, ny, nz), f32),
                pltpu.VMEM((STEPS, 2, 3, ny, nz), f32),
                pltpu.VMEM((STEPS, 2, 3, ny, nz), f32),
                pltpu.VMEM((n, tiles, rows, nz), f32),
                pltpu.VMEM((nc, xr + 2, ny, nz), f32),
                pltpu.VMEM((nc, xr + 2, ny, nz), f32),
                pltpu.VMEM((xr, ny, nz), f32),
                pltpu.VMEM((STEPS, xr, ny, nz), f32),
                pltpu.VMEM((n, tiles, rows, nz), f32),
                pltpu.VMEM((L, tiles, rows, nz), f32),
                pltpu.VMEM((L, tiles, rows, nz), f32),
                pltpu.VMEM((L, tiles, rows, nz), f32),
                dma((8,)),
                dma((2, 3, STEPS)),
                dma((2, 3, STEPS)),
                dma((n,)),
                dma((n,)),
                dma((1,)),
                dma((L,)),
                dma((L,)),
                dma((L,)),
                dma((L,)),
                dma((L,)),
                dma((L,)),
                dma((L,)),
            ],
            compiler_params=pltpu.CompilerParams(
                collective_id=0, has_side_effects=True, vmem_limit_bytes=56 * 1024 * 1024
            ),
        )(wavelet, encoding, cells, depth, data, fwd, adj, flat)
        fwd_out, adj_out, grad = pl.pallas_call(
            write_out,
            out_shape=(
                pltpu.HBM(fwd.shape, f32),
                pltpu.HBM(adj.shape, f32),
                pltpu.HBM(flat.shape, f32),
            ),
            in_specs=[vmem, vmem],
            out_specs=(hbm, hbm, hbm),
            scratch_shapes=[dma((5,))],
            compiler_params=pltpu.CompilerParams(vmem_limit_bytes=8 * 1024 * 1024),
        )(fields, grad)
        return fwd_out, adj_out, grad.reshape(mats.shape)

    return jax.shard_map(
        body,
        mesh=mesh,
        in_specs=(
            P("shot", None, "slab", None, None),
            P("shot", None, "slab", None, None),
            P(None, "slab", "shot", None),
            P(),
            P("shot", None),
            P("shot", None),
            P("slab", None),
            P("shot", None, "slab", None),
        ),
        out_specs=(
            P("shot", None, "slab", None, None),
            P("shot", None, "slab", None, None),
            P(None, "slab", "shot", None),
        ),
        check_vma=False,
    )
```

```python
import functools

import jax
import jax.numpy as jnp
from jax import lax
from jax.experimental import pallas as pl
from jax.experimental.pallas import tpu as pltpu
from jax.sharding import PartitionSpec as P

STEPS = 4
STEP_SIZE = 0.25
PAD = 8
VX, VY, VZ, SXX, SYY, SZZ, SYZ, SXZ, SXY = range(9)
PAIRS = [(0, 0), (0, 1), (0, 2), (1, 1), (1, 2), (2, 2), (3, 3), (4, 4), (5, 5)]


def kernel(
    n,
    slabs,
    scale,
    wavelet_in,
    encoding_in,
    cells_in,
    depth_in,
    data_in,
    fwd_in,
    adj_in,
    mats_in,
    F,
    grad_out,
    wavelet,
    encoding,
    cells,
    depth,
    data,
    up_out,
    dn_out,
    up_got,
    dn_got,
    slots,
    mat,
    acc,
    image,
    inj,
    blocks,
    ry,
    rright,
    rleft,
    load_sem,
    halo_send,
    halo_recv,
    ag_recv,
    ag_send_z,
    ag_send_o,
    ag_send_y,
    rs_recv_y,
    rs_send_y,
    rs_recv_r,
    rs_send_r,
    rs_recv_l,
    rs_send_l,
):
    _, comps, xr, ny, nz = fwd_in.shape
    tiles, rows, _ = mats_in.shape
    nc = mat.shape[0]
    yb = ny // n
    group = rows // yb
    L = n // 2
    me = lax.axis_index("shot")
    slab = lax.axis_index("slab")
    lo = lax.rem(me, 2)
    hi = me // 2
    partner = hi * 2 + 1 - lo

    small = [
        pltpu.make_async_copy(src, dst, load_sem.at[3 + i])
        for i, (src, dst) in enumerate(
            [
                (wavelet_in, wavelet),
                (encoding_in, encoding),
                (cells_in, cells),
                (depth_in, depth),
                (data_in, data),
            ]
        )
    ]
    loads = [
        pltpu.make_async_copy(fwd_in.at[0], F.at[0, :, pl.ds(1, xr), pl.ds(PAD, ny)], load_sem.at[0]),
        pltpu.make_async_copy(adj_in.at[0], F.at[1, :, pl.ds(1, xr), pl.ds(PAD, ny)], load_sem.at[1]),
        pltpu.make_async_copy(mats_in, slots.at[me], load_sem.at[2]),
    ]
    for c in loads + small:
        c.start()

    def get(w, c, x, by=0):
        return F[w, c, x, pl.ds(PAD + by, ny)]

    def put(w, c, x, value):
        F[w, c, x, pl.ds(PAD, ny)] = value

    zero_layer = jnp.zeros((ny, nz), jnp.float32)
    mat[0, 0] = zero_layer
    mat[0, xr + 1] = zero_layer
    for w in range(2):
        put(w, VX, 0, zero_layer)
        put(w, VY, xr + 1, zero_layer)
        put(w, VZ, xr + 1, zero_layer)
        for x in range(1, xr + 1):
            for c in (SXY, SYZ, VY):
                F[w, c, x, pl.ds(0, PAD)] = jnp.zeros((PAD, nz), jnp.float32)
            for c in (SYY, VX, VZ):
                F[w, c, x, pl.ds(PAD + ny, PAD)] = jnp.zeros((PAD, nz), jnp.float32)
        for i in range(3):
            for t in range(STEPS):
                up_got[t, w, i] = zero_layer
                dn_got[t, w, i] = zero_layer

    def shot_id(index):
        return {"shot": index}

    def slab_id(index):
        return {"slab": index}

    MESH = pl.DeviceIdType.MESH
    barrier = pltpu.get_barrier_semaphore()

    def greet(cond, device):
        @pl.when(cond)
        def _():
            pl.semaphore_signal(barrier, inc=1, device_id=device, device_id_type=MESH)

    has_r = hi < L - 1
    has_l = hi > 0
    has_up = slab < slabs - 1
    has_dn = slab > 0
    pl.semaphore_signal(barrier, inc=1, device_id=shot_id(partner), device_id_type=MESH)
    greet(has_r, shot_id(me + 2))
    greet(has_l, shot_id(me - 2))
    greet(has_up, slab_id(slab + 1))
    greet(has_dn, slab_id(slab - 1))
    one = jnp.int32(1)
    nul = jnp.int32(0)
    count = (
        one
        + jnp.where(has_r, one, nul)
        + jnp.where(has_l, one, nul)
        + jnp.where(has_up, one, nul)
        + jnp.where(has_dn, one, nul)
    )
    pl.semaphore_wait(barrier, count)

    def remote(src, dst, ss, rs, device):
        return pltpu.make_async_remote_copy(
            src_ref=src,
            dst_ref=dst,
            send_sem=ss,
            recv_sem=rs,
            device_id=device,
            device_id_type=MESH,
        )

    def when(cond, fn):
        pl.when(cond)(fn)

    def to_partner(block, src):
        return remote(
            src, slots.at[block], ag_send_y.at[block // 2], ag_recv.at[block], shot_id(partner)
        )

    def to_line(block, src, by, sem):
        return remote(src, slots.at[block], sem, ag_recv.at[block], shot_id(me + 2 * by))

    own_r = to_line(me, mats_in, 1, ag_send_z.at[me])
    own_l = to_line(me, mats_in, -1, ag_send_o.at[0])
    own_p = to_partner(me, mats_in)
    own_p.start()
    when(has_r, own_r.start)
    when(has_l, own_l.start)

    inner = pl.ds(PAD, ny)

    def halo(kind, t):
        if kind == 0:
            up_src, up_dst = up_out.at[t], up_got.at[t]
            dn_src, dn_dst = dn_out.at[t], dn_got.at[t]
        elif kind == 1:
            up_src, up_dst = F.at[:, VX, xr, inner], F.at[:, VX, 0, inner]
            dn_src = F.at[:, pl.ds(VY, 2), 1, inner]
            dn_dst = F.at[:, pl.ds(VY, 2), xr + 1, inner]
        else:
            up_src, up_dst = mat.at[0, xr], mat.at[0, 0]
            dn_src, dn_dst = mat.at[0, 1], mat.at[0, xr + 1]
        up = remote(
            up_src, up_dst, halo_send.at[0, kind, t], halo_recv.at[0, kind, t], slab_id(slab + 1)
        )
        dn = remote(
            dn_src, dn_dst, halo_send.at[1, kind, t], halo_recv.at[1, kind, t], slab_id(slab - 1)
        )
        return up, dn

    def halo_start(kind, t):
        up, dn = halo(kind, t)
        when(has_up, up.start)
        when(has_dn, dn.start)

    def halo_wait(kind, t):
        up, dn = halo(kind, t)
        when(has_dn, up.wait_recv)
        when(has_up, dn.wait_recv)

    def halo_sent(kind, t):
        up, dn = halo(kind, t)
        when(has_up, up.wait_send)
        when(has_dn, dn.wait_send)

    for c in loads + small:
        c.wait()
    halo_start(1, 0)

    lane = lax.broadcasted_iota(jnp.int32, (ny, nz), 1)
    row = lax.broadcasted_iota(jnp.int32, (ny, nz), 0)

    def up_y(w, c, x):
        return get(w, c, x, 1) - get(w, c, x)

    def down_y(w, c, x):
        return get(w, c, x) - get(w, c, x, -1)

    def up_z(a):
        return jnp.where(lane == nz - 1, 0.0, pltpu.roll(a, nz - 1, 1)) - a

    def down_z(a):
        return a - jnp.where(lane == 0, 0.0, pltpu.roll(a, 1, 1))

    def pack(t):
        for w in range(2):
            sxz = get(w, SXZ, xr)
            up_out[t, w, 0] = down_y(w, SXY, xr) + down_z(sxz) - get(w, SXX, xr)
            up_out[t, w, 1] = sxz
            up_out[t, w, 2] = get(w, SXY, xr)
            dn_out[t, w, 0] = get(w, SXY, 1) + up_y(w, SYY, 1) + down_z(get(w, SYZ, 1))
            dn_out[t, w, 1] = get(w, SXZ, 1) + down_y(w, SYZ, 1) + up_z(get(w, SZZ, 1))
            dn_out[t, w, 2] = get(w, SXX, 1)
        halo_start(0, t)

    def unpack(t):
        halo_wait(0, t)
        for w in range(2):
            put(w, SXZ, 0, up_got[t, w, 1])
            put(w, SXY, 0, up_got[t, w, 2])
            put(w, SXX, xr + 1, dn_got[t, w, 2])

    def ghosts(t):
        top = xr + 1
        for w in range(2):
            fx = get(w, SXX, 1) + up_got[t, w, 0]
            fy = dn_got[t, w, 0] - get(w, SXY, xr)
            fz = dn_got[t, w, 1] - get(w, SXZ, xr)
            put(w, VX, 0, get(w, VX, 0) + mat[0, 0] * fx)
            put(w, VY, top, get(w, VY, top) + mat[0, top] * fy)
            put(w, VZ, top, get(w, VZ, top) + mat[0, top] * fz)

    pack(0)

    eye = lax.broadcasted_iota(jnp.int32, (ny, ny), 0) == lax.broadcasted_iota(
        jnp.int32, (ny, ny), 1
    )

    def column(r):
        wide = jnp.broadcast_to(r, (ny, ny))
        return jnp.sum(jnp.where(eye, wide, 0.0), axis=1, keepdims=True)

    def prepare(x, carry):
        cell = ((slab * xr + x) * ny + row) * nz + lane
        total = jnp.zeros((ny, nz), jnp.float32)
        for j in range(cells.shape[1]):
            sign = (2 * encoding[0, j] - 1).astype(jnp.float32)
            total = total + jnp.where(cell == cells[0, j], sign, 0.0)
        image[x] = total
        hit = lane.astype(jnp.float32) == column(depth[pl.ds(x, 1), :].astype(jnp.float32))
        for t in range(STEPS):
            inj[t, x] = jnp.where(hit, column(data[0, t, pl.ds(x, 1), :]), 0.0)
        return carry

    lax.fori_loop(0, xr, prepare, 0)

    for k in range(1, L):
        def right_moving(k=k):
            b = me - 2 * k
            ref = slots.at[b]
            to_line(b, ref, 1, ag_send_z.at[b]).wait_recv()
            to_partner(b, ref).start()
            when(has_r, to_line(b, ref, 1, ag_send_z.at[b]).start)

        def left_moving(k=k):
            b = me + 2 * k
            ref = slots.at[b]
            to_line(b, ref, -1, ag_send_z.at[b]).wait_recv()
            to_partner(b, ref).start()
            when(has_l, to_line(b, ref, -1, ag_send_z.at[b]).start)

        when(hi >= k, right_moving)
        when(hi + k < L, left_moving)
    for h in range(L):
        b = h * 2 + 1 - lo
        to_partner(b, slots.at[b]).wait_recv()

    def assemble(xg, carry):
        for c in range(nc):
            held = [slots[i, c * (xr // group) + xg] for i in range(n)]
            for j in range(group):
                whole = jnp.concatenate([h[j * yb : (j + 1) * yb] for h in held], axis=0)
                mat[c, xg * group + j + 1] = whole * STEP_SIZE
        return carry

    lax.fori_loop(0, xr // group, assemble, 0)
    halo_start(2, 0)

    def velocity_layer(t, x):
        forces = []
        old = []
        for w in range(2):
            sxx, sxy, sxz = get(w, SXX, x), get(w, SXY, x), get(w, SXZ, x)
            syz = get(w, SYZ, x)
            fx = (get(w, SXX, x + 1) - sxx) + down_y(w, SXY, x) + down_z(sxz)
            fy = (sxy - get(w, SXY, x - 1)) + up_y(w, SYY, x) + down_z(syz)
            fz = (sxz - get(w, SXZ, x - 1)) + down_y(w, SYZ, x) + up_z(get(w, SZZ, x))
            forces.append([fx, fy, fz])
            old.append([get(w, VX, x), get(w, VY, x), get(w, VZ, x)])
        term = (
            forces[0][0] * old[1][0] + forces[0][1] * old[1][1] + forces[0][2] * old[1][2]
        )
        acc[0, x] = term if t == 0 else acc[0, x] + term
        buoy = mat[0, x]
        for w in range(2):
            for c in range(3):
                put(w, c, x, old[w][c] + buoy * forces[w][c])

    def strain_of(w, x):
        vx, vy, vz = get(w, VX, x), get(w, VY, x), get(w, VZ, x)
        return [
            vx - get(w, VX, x - 1),
            down_y(w, VY, x),
            down_z(vz),
            up_z(vy) + up_y(w, VZ, x),
            up_z(vx) + (get(w, VZ, x + 1) - vz),
            up_y(w, VX, x) + (get(w, VY, x + 1) - vy),
        ]

    def add_terms(t, x, f, a):
        for i, (p, q) in enumerate(PAIRS):
            term = f[p] * a[q]
            if p != q:
                term = term + f[q] * a[p]
            if t > 0:
                term = term + acc[i + 1, x]
            acc[i + 1, x] = term

    def put_blocks(xg):
        for c in range(nc):
            held = [acc[c, xg * group + j + 1] * scale for j in range(group)]
            for i in range(n):
                blocks[i, c * (xr // group) + xg] = jnp.concatenate(
                    [h[i * yb : (i + 1) * yb] for h in held], axis=0
                )

    def stress_layer(t, x, strains):
        m = [mat[c, x] for c in range(nc)]
        for w in range(2):
            exx, eyy, ezz, gyz, gxz, gxy = strains[w]
            extra = wavelet[t] * image[x - 1] if w == 0 else inj[t, x - 1]
            for c, change in (
                (SXX, m[1] * exx + m[2] * eyy + m[3] * ezz),
                (SYY, m[2] * exx + m[4] * eyy + m[5] * ezz),
                (SZZ, m[3] * exx + m[5] * eyy + m[6] * ezz + extra),
                (SYZ, m[7] * gyz),
                (SXZ, m[8] * gxz),
                (SXY, m[9] * gxy),
            ):
                put(w, c, x, get(w, c, x) + change)

    def over(start, stop, step, fn):
        def one_layer(j, carry):
            fn(start + j * step)
            return carry

        lax.fori_loop(0, (stop - start + step - 1) // step, one_layer, 0, unroll=2)

    def interior(fn):
        over(2, xr, 1, fn)

    def rims(fn):
        over(1, xr + 1, xr - 1, fn)

    for t in range(STEPS):
        last = t == STEPS - 1
        interior(functools.partial(velocity_layer, t))
        unpack(t)
        if t == 0:
            halo_sent(1, 0)
        rims(functools.partial(velocity_layer, t))
        if t == 0:
            halo_wait(1, 0)
            halo_wait(2, 0)
        ghosts(t)

        def both(x, t=t, last=last):
            strains = [strain_of(w, x) for w in range(2)]
            add_terms(t, x, strains[0], strains[1])
            if not last:
                stress_layer(t, x, strains)

        rims(both)
        if not last:
            pack(t + 1)
        interior(both)
    over(0, xr // group, 1, put_blocks)

    def rs_y(d):
        return remote(
            blocks.at[d * 2 + 1 - lo],
            ry.at[d],
            rs_send_y.at[d],
            rs_recv_y.at[d],
            shot_id(partner),
        )

    def rs_r(d):
        return remote(
            ry.at[d], rright.at[d], rs_send_r.at[d], rs_recv_r.at[d], shot_id(me + 2)
        )

    def rs_l(d):
        return remote(ry.at[d], rleft.at[d], rs_send_l.at[d], rs_recv_l.at[d], shot_id(me - 2))

    for k in range(L - 1, 0, -1):
        when(hi + k < L, lambda k=k: rs_y(hi + k).start())
        when(hi >= k, lambda k=k: rs_y(hi - k).start())
    rs_y(hi).start()

    over(1, xr + 1, 1, lambda x: stress_layer(STEPS - 1, x, [strain_of(w, x) for w in range(2)]))

    def add_into(d, extra, target):
        def one_layer(x, carry):
            for c in range(nc):
                i = x * nc + c
                total = ry[d, i] + blocks[d * 2 + lo, i]
                if extra is not None:
                    total = total + extra[d, i]
                target[i] = total
            return carry

        lax.fori_loop(0, tiles // nc, one_layer, 0)

    for k in range(L - 1, 0, -1):
        def send_right(k=k):
            d = hi + k
            rs_y(d).wait_recv()

            def plus():
                rs_r(d).wait_recv()
                add_into(d, rright, ry.at[d])

            when(has_l, plus)
            when(hi == 0, lambda: add_into(d, None, ry.at[d]))
            rs_r(d).start()

        def send_left(k=k):
            d = hi - k
            rs_y(d).wait_recv()

            def plus():
                rs_l(d).wait_recv()
                add_into(d, rleft, ry.at[d])

            when(has_r, plus)
            when(hi == L - 1, lambda: add_into(d, None, ry.at[d]))
            rs_l(d).start()

        when(hi + k < L, send_right)
        when(hi >= k, send_left)

    rs_y(hi).wait_recv()
    add_into(hi, None, grad_out)

    def take(ref):
        def one_layer(x, carry):
            for c in range(nc):
                i = x * nc + c
                grad_out[i] = grad_out[i] + ref[hi, i]
            return carry

        lax.fori_loop(0, tiles // nc, one_layer, 0)

    def from_left():
        rs_r(hi).wait_recv()
        take(rright)

    def from_right():
        rs_l(hi).wait_recv()
        take(rleft)

    when(has_l, from_left)
    when(has_r, from_right)

    when(has_r, own_r.wait_send)
    when(has_l, own_l.wait_send)
    own_p.wait_send()
    for k in range(1, L):
        def right_sent(k=k):
            b = me - 2 * k
            when(has_r, to_line(b, slots.at[b], 1, ag_send_z.at[b]).wait_send)
            to_partner(b, slots.at[b]).wait_send()

        def left_sent(k=k):
            b = me + 2 * k
            when(has_l, to_line(b, slots.at[b], -1, ag_send_z.at[b]).wait_send)
            to_partner(b, slots.at[b]).wait_send()

        when(hi >= k, right_sent)
        when(hi + k < L, left_sent)
        when(hi + k < L, lambda k=k: rs_y(hi + k).wait_send())
        when(hi >= k, lambda k=k: rs_y(hi - k).wait_send())
        when(hi + k < L, lambda k=k: rs_r(hi + k).wait_send())
        when(hi >= k, lambda k=k: rs_l(hi - k).wait_send())
    rs_y(hi).wait_send()
    for t in range(STEPS):
        halo_sent(0, t)
    halo_sent(2, 0)


def write_out(F, grad, fwd_out, adj_out, grad_out, sem):
    xr, ny = fwd_out.shape[2:4]
    comps = fwd_out.shape[1]
    half = comps // 2
    copies = [pltpu.make_async_copy(grad, grad_out, sem.at[4])]
    for w, out in ((0, fwd_out), (1, adj_out)):
        for j, (first, count) in enumerate(((0, half), (half, comps - half))):
            copies.append(
                pltpu.make_async_copy(
                    F.at[w, pl.ds(first, count), pl.ds(1, xr), pl.ds(PAD, ny)],
                    out.at[0, pl.ds(first, count)],
                    sem.at[2 * w + j],
                )
            )
    for c in copies:
        c.start()
    for c in copies:
        c.wait()


def solution(mesh):
    n = mesh.shape["shot"]
    slabs = mesh.shape["slab"]

    def body(fwd, adj, mats, wavelet, encoding, cells, depth, data):
        shots, comps, xr, ny, nz = fwd.shape
        nc, _, yb, _ = mats.shape
        L = n // 2
        scale = float(shots * n * STEPS) ** (-0.5)
        rows = max(8, yb)
        tiles = nc * xr * yb // rows
        flat = mats.reshape(tiles, rows, nz)
        vmem = pl.BlockSpec(memory_space=pltpu.VMEM)
        hbm = pl.BlockSpec(memory_space=pltpu.HBM)
        any_spec = pl.BlockSpec(memory_space=pl.ANY)
        dma = pltpu.SemaphoreType.DMA
        f32 = jnp.float32
        fields, grad = pl.pallas_call(
            functools.partial(kernel, n, slabs, scale),
            out_shape=(
                pltpu.VMEM((2, comps, xr + 2, ny + 2 * PAD, nz), f32),
                pltpu.VMEM(flat.shape, f32),
            ),
            in_specs=[any_spec] * 8,
            out_specs=(vmem, vmem),
            scratch_shapes=[
                pltpu.SMEM(wavelet.shape, f32),
                pltpu.SMEM(encoding.shape, jnp.int32),
                pltpu.SMEM(cells.shape, jnp.int32),
                pltpu.VMEM(depth.shape, jnp.int32),
                pltpu.VMEM(data.shape, f32),
                pltpu.VMEM((STEPS, 2, 3, ny, nz), f32),
                pltpu.VMEM((STEPS, 2, 3, ny, nz), f32),
                pltpu.VMEM((STEPS, 2, 3, ny, nz), f32),
                pltpu.VMEM((STEPS, 2, 3, ny, nz), f32),
                pltpu.VMEM((n, tiles, rows, nz), f32),
                pltpu.VMEM((nc, xr + 2, ny, nz), f32),
                pltpu.VMEM((nc, xr + 2, ny, nz), f32),
                pltpu.VMEM((xr, ny, nz), f32),
                pltpu.VMEM((STEPS, xr, ny, nz), f32),
                pltpu.VMEM((n, tiles, rows, nz), f32),
                pltpu.VMEM((L, tiles, rows, nz), f32),
                pltpu.VMEM((L, tiles, rows, nz), f32),
                pltpu.VMEM((L, tiles, rows, nz), f32),
                dma((8,)),
                dma((2, 3, STEPS)),
                dma((2, 3, STEPS)),
                dma((n,)),
                dma((n,)),
                dma((1,)),
                dma((L,)),
                dma((L,)),
                dma((L,)),
                dma((L,)),
                dma((L,)),
                dma((L,)),
                dma((L,)),
            ],
            compiler_params=pltpu.CompilerParams(
                collective_id=0, has_side_effects=True, vmem_limit_bytes=56 * 1024 * 1024
            ),
        )(wavelet, encoding, cells, depth, data, fwd, adj, flat)
        fwd_out, adj_out, grad = pl.pallas_call(
            write_out,
            out_shape=(
                pltpu.HBM(fwd.shape, f32),
                pltpu.HBM(adj.shape, f32),
                pltpu.HBM(flat.shape, f32),
            ),
            in_specs=[vmem, vmem],
            out_specs=(hbm, hbm, hbm),
            scratch_shapes=[dma((5,))],
            compiler_params=pltpu.CompilerParams(vmem_limit_bytes=8 * 1024 * 1024),
        )(fields, grad)
        return fwd_out, adj_out, grad.reshape(mats.shape)

    return jax.shard_map(
        body,
        mesh=mesh,
        in_specs=(
            P("shot", None, "slab", None, None),
            P("shot", None, "slab", None, None),
            P(None, "slab", "shot", None),
            P(),
            P("shot", None),
            P("shot", None),
            P("slab", None),
            P("shot", None, "slab", None),
        ),
        out_specs=(
            P("shot", None, "slab", None, None),
            P("shot", None, "slab", None, None),
            P(None, "slab", "shot", None),
        ),
        check_vma=False,
    )
```
